128 devices in a mesh: ctx: 8 (over y, core), tp: 8 (over x, z_hi), dp: 2 (over z_lo).
Axes of the slice: x: 4, y: 4, z: 4 (z_hi: 2, z_lo: 2; z = z_hi * 2 + z_lo), core: 2. Of those that a mesh axis runs over, the one named last changes fastest.
Arguments:
- signal_first: bfloat16 [131072, 128], P(('ctx', 'tp', 'dp')), may hold values from -6 to 6
- gate_first: bfloat16 [131072, 128], P(('ctx', 'tp', 'dp')), may hold values from -6 to 6
- signal_second: bfloat16 [131072, 128], P(('ctx', 'tp', 'dp')), may hold values from -6 to 6
- gate_second: bfloat16 [131072, 128], P(('ctx', 'tp', 'dp')), may hold values from -6 to 6
- upstream_second: bfloat16 [131072, 128], P(('ctx', 'tp', 'dp')), may hold values from -6 to 6
- filter_param: bfloat16 [131072, 128], P(('ctx', 'tp', 'dp')), may hold values from -6 to 6
Outputs:
- mixed_first: bfloat16 [131072, 128], P(('ctx', 'tp', 'dp'))
- signal_grad: bfloat16 [131072, 128], P(('ctx', 'tp', 'dp'))
- gate_grad: bfloat16 [131072, 128], P(('ctx', 'tp', 'dp'))
- filter_grad: float32 [131072, 128], P(('ctx', 'tp', 'dp'))
The draws below stay inside these ranges and needn't reach their ends.
All inputs are finite; a program needn't handle non-finite values.
Results may differ from the reference program's by a relative error of at most 0.0049.
Values may be sent and summed in bfloat16 or wider, within the bound.
No kernel may reach another device: no remote copies, remote signals or barrier semaphores. Data moves between devices by JAX's collectives and lax.ppermute only.
A program may use at most 128 MiB of HBM per device.

```python
import math
import jax
import jax.numpy as jnp

FA = 512
FB = 512
SEQ = 131072
CH = 128


def steps_of(stream_key, dims, shards, smallest, top_value):
    loudness, own = 1.0, jax.random.fold_in(stream_key, 6)
    for position, parts in shards:
        steps = jnp.exp(jax.random.uniform(jax.random.fold_in(own, position), (parts,), jnp.float32, smallest / len(shards), top_value / len(shards)))
        loudness = loudness * jnp.repeat(steps, dims[position] // parts).reshape([-1 if axis == position else 1 for axis in range(len(dims))])
    return loudness


def gaussian(own_key, dims, spread, bound, cuts=(), kind=jnp.bfloat16):
    level = steps_of(own_key, dims, cuts, -0.22, 0.18) if cuts else 1.0
    drawn = jax.random.normal(own_key, dims, jnp.float32) * spread * level
    return jnp.minimum(jnp.maximum(drawn, -bound), bound).astype(kind)


def setup_inputs(seed: int = 0) -> dict:
    streams_of = jax.random.split(jax.random.key(seed), 7)
    signal_first = gaussian(streams_of[0], (SEQ, CH), 1.0, 6.0, ((0, 128),))
    gate_first = gaussian(streams_of[1], (SEQ, CH), 1.0, 6.0, ((0, 128),))
    signal_second = gaussian(streams_of[2], (SEQ, CH), 1.0, 6.0, ((0, 128),))
    gate_second = gaussian(streams_of[3], (SEQ, CH), 1.0, 6.0, ((0, 128),))
    upstream_second = gaussian(streams_of[4], (SEQ, CH), 1.0, 6.0, ((0, 128),))
    filter_param = gaussian(streams_of[5], (SEQ, CH), 1.0, 6.0, ((0, 128),))
    return {"signal_first": signal_first, "gate_first": gate_first, "signal_second": signal_second, "gate_second": gate_second, "upstream_second": upstream_second, "filter_param": filter_param}


def spectrum(values, total):
    return jnp.fft.rfft(values.astype(jnp.float32), n=total, axis=0)

def inverse_part(spec, total, length):
    return jnp.fft.irfft(spec, n=total, axis=0)[:length]

def reference(signal_first, gate_first, signal_second, gate_second, upstream_second, filter_param):
    period = FA * FB
    gain_scale = 1.0 / math.sqrt(SEQ)
    filter_spec = gain_scale * spectrum(filter_param, period)
    conv_first = inverse_part(filter_spec * spectrum(signal_first, period), period, SEQ)
    mixed_first = (gate_first.astype(jnp.float32) * conv_first).astype(jnp.bfloat16)
    second_spec = spectrum(signal_second, period)
    conv_second = inverse_part(filter_spec * second_spec, period, SEQ)
    gate_grad = (upstream_second.astype(jnp.float32) * conv_second).astype(jnp.bfloat16)
    grad_mid = (gate_second.astype(jnp.float32) * upstream_second.astype(jnp.float32)).astype(jnp.bfloat16)
    middle_spec = spectrum(grad_mid, period)
    signal_grad = inverse_part(jnp.conj(filter_spec) * middle_spec, period, SEQ).astype(jnp.bfloat16)
    filter_grad = gain_scale * inverse_part(middle_spec * jnp.conj(second_spec), period, SEQ)
    return (mixed_first, signal_grad, gate_grad, filter_grad)
```

```python
import functools
import math

import jax
import jax.numpy as jnp
import ml_dtypes
import numpy as np
from jax import lax
from jax.experimental import pallas as pl
from jax.experimental.pallas import tpu as pltpu
from jax.sharding import PartitionSpec as P

AXES = ("ctx", "tp", "dp")
SEQ = 131072
ROWS = 8
LANES = 128
FIRST = 1024
SECOND = 128
HALF = FIRST // 2
QUARTER = FIRST // 4
CHUNK = 64
STEPS = QUARTER // CHUNK
BLOCK = 4 * CHUNK
ARRAYS = 4
PIECE = ARRAYS * ROWS
PAIR = 2 * ROWS
STRIDE = ROWS + 1
BACK = FIRST
FORWARD_SECOND = BACK + FIRST
INVERSE_SECOND = FORWARD_SECOND + 2 * SECOND
TABLE_WIDTH = INVERSE_SECOND + 2 * SECOND
SECOND_SCALE = 1.66569
BF16 = jnp.bfloat16
F32 = jnp.float32


@functools.cache
def make_tables():
    quarter = QUARTER * np.arange(4).reshape(1, 4, 1)
    first = (np.arange(QUARTER).reshape(STEPS, 1, CHUNK) + quarter).reshape(FIRST)
    position, second = np.arange(FIRST), np.arange(SECOND)
    product = (4 * first[:, None] + 1) * (2 * position[None, :] + 1) % (8 * FIRST)
    first_phase = 2 * np.pi * product / (8 * FIRST)
    twist_phase = 2 * np.pi * (4 * first[:, None] + 1) * (second[None, :] - SECOND // 2) / (4 * SEQ)
    forward_phase = twist_phase + np.pi / 4 * (first // QUARTER)[:, None]
    second_phase = 2 * np.pi * ((second[:, None] * second[None, :]) % SECOND) / SECOND
    scale = (SEQ * math.sqrt(SEQ) * SECOND_SCALE**3 * math.sqrt(2.0)) ** (-1 / 3)
    back = [np.cos(twist_phase) + np.sin(twist_phase), np.cos(twist_phase) - np.sin(twist_phase)]
    twist = scale * np.concatenate([np.cos(forward_phase), np.sin(forward_phase)] + back, axis=1)
    cos_second, sin_second = np.cos(second_phase), np.sin(second_phase)
    forward_second = np.block([[cos_second, sin_second], [-sin_second, cos_second]])
    inverse_second = np.block([[cos_second, -sin_second], [sin_second, cos_second]])

    columns = position.reshape(QUARTER, 4).T.reshape(FIRST)
    lowest = first_phase.reshape(STEPS // 2, 2, 4, CHUNK, FIRST)[:, :, 0].reshape(STEPS // 2, 2 * CHUNK, FIRST)
    lowest = lowest[:, :, columns]
    joined = np.zeros((FIRST, TABLE_WIDTH), ml_dtypes.bfloat16)
    joined[:HALF, :FIRST] = np.concatenate([np.cos(lowest), np.sin(lowest)], axis=1).reshape(HALF, FIRST)
    half_phase = first_phase[:, :HALF].T
    joined[:HALF, BACK : BACK + FIRST] = np.cos(half_phase - np.pi / 4)
    joined[HALF:, BACK : BACK + FIRST] = np.cos(half_phase + np.pi / 4)
    for column, table in ((FORWARD_SECOND, forward_second), (INVERSE_SECOND, inverse_second)):
        table = SECOND_SCALE * np.concatenate([table, table], axis=0)
        joined[: 4 * SECOND, column : column + 2 * SECOND] = table
    return joined, twist.astype(np.float32)


def pack_kernel(filter_hbm, first_hbm, second_hbm, gate_hbm, upstream_hbm, out_ref, local, scratch, sems):
    sources = (filter_hbm, first_hbm, second_hbm, gate_hbm, upstream_hbm)
    copies = [
        pltpu.make_async_copy(source, local.at[index], sems.at[index])
        for index, source in enumerate(sources)
    ]
    for copy in copies:
        copy.start()
    for index in range(ARRAYS):
        copies[index].wait()
        if index == ARRAYS - 1:
            copies[ARRAYS].wait()
        for row in range(ROWS):
            span = pl.ds(row * LANES, LANES)
            block = local[index, span, :]
            if index == ARRAYS - 1:
                block = (block.astype(F32) * local[ARRAYS, span, :].astype(F32)).astype(BF16)
            scratch[index, pl.ds(row, LANES, stride=STRIDE), :] = block.T.astype(F32)
        if index % 2:
            for channel in range(LANES):
                rows = pl.ds(channel * STRIDE, ROWS)
                pair = jnp.concatenate([scratch[index - 1, rows, :], scratch[index, rows, :]], axis=0)
                out_ref[channel, index // 2 * PAIR : (index // 2 + 1) * PAIR, :] = pair.astype(BF16)


def unpack_kernel(
    in_ref, gate_ref, upstream_ref, mixed_hbm, signal_hbm, gate_out_hbm, filter_hbm,
    scratch, halves, filter_out, sems,
):
    mirrored = lax.axis_index("ctx") >= lax.axis_size("ctx") // 2
    targets = (mixed_hbm, gate_out_hbm, signal_hbm, filter_hbm)
    copies = []
    for index in (3, 2, 0, 1):
        if index in (3, 0):
            for channel in range(LANES):
                pair = in_ref[channel, index // 2 * PAIR : (index // 2 + 1) * PAIR, :].astype(F32)
                rows = pl.ds(channel * STRIDE, ROWS)
                scratch[index // 2 * 2, rows, :] = pair[:ROWS]
                scratch[index // 2 * 2 + 1, rows, :] = pair[ROWS:]
        for row in range(ROWS):
            place = jnp.where(mirrored, ROWS - 1 - row, row)
            span = pl.ds(pl.multiple_of(place * LANES, LANES), LANES)
            block = scratch[index, pl.ds(row, LANES, stride=STRIDE), :]
            block = block.astype(BF16).T.astype(F32)
            if index == 0:
                halves[index, span, :] = (gate_ref[span, :].astype(F32) * block).astype(BF16)
            elif index == 1:
                halves[index, span, :] = (upstream_ref[span, :].astype(F32) * block).astype(BF16)
            elif index == 2:
                halves[index, span, :] = block.astype(BF16)
            else:
                filter_out[span, :] = block
        source = filter_out if index == 3 else halves.at[index]
        copies.append(pltpu.make_async_copy(source, targets[index], sems.at[index]))
        copies[-1].start()
    for copy in copies:
        copy.wait()


def two_pass(real, imag, table_ref, column):
    real_high, imag_high = real.astype(BF16), imag.astype(BF16)
    real_low = (real - real_high.astype(F32)).astype(BF16)
    imag_low = (imag - imag_high.astype(F32)).astype(BF16)
    joined = jnp.concatenate([real_high, imag_high, real_low, imag_low], axis=1)
    table = table_ref[: 4 * SECOND, column : column + 2 * SECOND]
    out = jnp.dot(joined, table, preferred_element_type=F32)
    return out[:, :SECOND], out[:, SECOND:]


def convolve_kernel(in_ref, table_ref, twist_ref, out_ref, rows_ref, values_ref, sum_ref, difference_ref):
    lanes = [slice(index * LANES, (index + 1) * LANES) for index in range(ARRAYS)]
    pairs = [slice(start, start + 2 * LANES) for start in range(0, ARRAYS * LANES, 2 * LANES)]

    def lay_out(pair):
        arrived = in_ref[:, pair * PAIR : (pair + 1) * PAIR, :].astype(F32)
        for index in range(2):
            part = lanes[2 * pair + index]
            rows_ref[2 * pair + index] = arrived[:, index * ROWS : (index + 1) * ROWS, :].reshape(FIRST, LANES)
            for residue in range(4):
                values_ref[residue * QUARTER : (residue + 1) * QUARTER, part] = (
                    rows_ref[2 * pair + index, pl.ds(residue, QUARTER, stride=4), :].astype(BF16)
                )

    def rows_of(step):
        return slice(step * BLOCK, (step + 1) * BLOCK)

    def first_factor(double, pair):
        rows = rows_of(double)
        p0, p1, p2, p3 = (
            jnp.dot(
                table_ref[rows, residue * QUARTER : (residue + 1) * QUARTER],
                values_ref[residue * QUARTER : (residue + 1) * QUARTER, pairs[pair]],
                preferred_element_type=F32,
            )
            for residue in range(4)
        )
        s02, d02, s13, d13 = p0 + p2, p0 - p2, p1 + p3, p1 - p3
        real, imag = slice(0, 2 * CHUNK), slice(2 * CHUNK, 4 * CHUNK)
        reals = [s02[real] + s13[real], d02[real] - d13[imag], s02[real] - s13[real], d02[real] + d13[imag]]
        imags = [s02[imag] + s13[imag], d02[imag] + d13[real], s02[imag] - s13[imag], d02[imag] - d13[real]]
        return [
            tuple(
                jnp.concatenate([value[step * CHUNK : (step + 1) * CHUNK] for value in values], axis=0)
                for values in (reals, imags)
            )
            for step in range(2)
        ]

    def second_factor(step, turned):
        real, imag = (jnp.concatenate(parts, axis=1) for parts in zip(*turned))
        cos_twist, sin_twist = twist_ref[rows_of(step), :SECOND], twist_ref[rows_of(step), SECOND : 2 * SECOND]
        return [
            two_pass(
                real[:, part] * cos_twist - imag[:, part] * sin_twist,
                real[:, part] * sin_twist + imag[:, part] * cos_twist,
                table_ref,
                FORWARD_SECOND,
            )
            for part in lanes
        ]

    def multiply(spectra):
        (fr, fi), (ar, ai), (br, bi), (mr, mi) = spectra
        products = [
            (fr * ar - fi * ai, fr * ai + fi * ar),
            (fr * br - fi * bi, fr * bi + fi * br),
            (fr * mr + fi * mi, fr * mi - fi * mr),
            (mr * br + mi * bi, mi * br - mr * bi),
        ]
        return [two_pass(real, imag, table_ref, INVERSE_SECOND) for real, imag in products]

    def store(step, results):
        sum_twist = twist_ref[rows_of(step), 2 * SECOND : 3 * SECOND]
        difference_twist = twist_ref[rows_of(step), 3 * SECOND :]
        for part, (real, imag) in zip(lanes, results):
            sum_ref[rows_of(step), part] = (real * difference_twist + imag * sum_twist).astype(BF16)
            difference_ref[rows_of(step), part] = (real * sum_twist - imag * difference_twist).astype(BF16)

    step = HALF // 4
    count = step // ROWS
    early = rows_of(STEPS - 3).stop

    def way_back(part, rows):
        columns = slice(BACK + rows.start, BACK + rows.stop)
        even = jnp.dot(
            table_ref[part * step : (part + 1) * step, columns], sum_ref[rows, :], preferred_element_type=F32
        )
        odd = jnp.dot(
            table_ref[HALF + part * step : HALF + (part + 1) * step, columns],
            difference_ref[rows, :],
            preferred_element_type=F32,
        )
        return even, odd

    turned, spectra, results, partial = {}, {}, {}, {}

    def begin(double, pair):
        for index, value in enumerate(first_factor(double, pair)):
            turned.setdefault(2 * double + index, []).append(value)

    for pair in range(2):
        lay_out(pair)
        begin(0, pair)
    for turn in range(1, STEPS + 3):
        if turn % 2 and turn + 1 < STEPS:
            for pair in range(2):
                begin((turn + 1) // 2, pair)
        if 0 <= turn - 1 < STEPS:
            spectra[turn - 1] = second_factor(turn - 1, turned.pop(turn - 1))
        if turn > STEPS:
            for part in range(2 * (turn - STEPS - 1), 2 * (turn - STEPS)):
                partial[part] = way_back(part, slice(0, early))
        if 0 <= turn - 2 < STEPS:
            results[turn - 2] = multiply(spectra.pop(turn - 2))
        if 0 <= turn - 3 < STEPS:
            store(turn - 3, results.pop(turn - 3))

    for part in range(HALF // step):
        even, odd = way_back(part, slice(early, FIRST))
        even, odd = even + partial[part][0], odd + partial[part][1]
        for result, places in (
            (even + odd, range(part * count, (part + 1) * count)),
            (even - odd, range(LANES - 1 - part * count, LANES - 1 - (part + 1) * count, -1)),
        ):
            pieces = [result[:, lane].reshape(count, ROWS, LANES) for lane in lanes]
            joined = jnp.concatenate(pieces, axis=1).astype(BF16)
            for index, place in enumerate(places):
                out_ref[place] = joined[index]


def vmem():
    return pl.BlockSpec(memory_space=pltpu.VMEM)


def hbm():
    return pl.BlockSpec(memory_space=pltpu.HBM)


def exchange(pieces):
    return lax.all_to_all(pieces, AXES, split_axis=0, concat_axis=0, tiled=True)


def on_device(signal_first, gate_first, signal_second, gate_second, upstream_second, filter_param):
    positions = ROWS * LANES
    local = jax.ShapeDtypeStruct((positions, LANES), BF16)
    pieces = jax.ShapeDtypeStruct((LANES, PIECE, LANES), BF16)
    sources = (filter_param, signal_first, signal_second, gate_second, upstream_second)
    packed = pl.pallas_call(
        pack_kernel,
        out_shape=pieces,
        in_specs=[hbm()] * 5,
        out_specs=vmem(),
        scratch_shapes=[
            pltpu.VMEM((5, positions, LANES), BF16),
            pltpu.VMEM((ARRAYS, STRIDE * LANES, LANES), F32),
            pltpu.SemaphoreType.DMA((5,)),
        ],
        compiler_params=pltpu.CompilerParams(vmem_limit_bytes=40 * 1024 * 1024),
        cost_estimate=pl.CostEstimate(flops=20_000_000_000, bytes_accessed=2_400_000, transcendentals=0),
        name="pack",
    )(*[pltpu.with_memory_space_constraint(value, pltpu.HBM) for value in sources])
    convolved = pl.pallas_call(
        convolve_kernel,
        out_shape=pieces,
        in_specs=[vmem()] * 3,
        out_specs=vmem(),
        scratch_shapes=[pltpu.VMEM((ARRAYS, FIRST, LANES), F32)]
        + [pltpu.VMEM((FIRST, ARRAYS * LANES), BF16)] * 3,
        compiler_params=pltpu.CompilerParams(vmem_limit_bytes=40 * 1024 * 1024),
        name="convolve",
    )(exchange(packed), *make_tables())
    return pl.pallas_call(
        unpack_kernel,
        out_shape=(local, local, local, jax.ShapeDtypeStruct((positions, LANES), F32)),
        in_specs=[vmem()] * 3,
        out_specs=(hbm(),) * 4,
        scratch_shapes=[
            pltpu.VMEM((ARRAYS, STRIDE * LANES, LANES), F32),
            pltpu.VMEM((3, positions, LANES), BF16),
            pltpu.VMEM((positions, LANES), F32),
            pltpu.SemaphoreType.DMA((ARRAYS,)),
        ],
        compiler_params=pltpu.CompilerParams(vmem_limit_bytes=40 * 1024 * 1024),
        name="unpack",
    )(exchange(convolved), gate_first, upstream_second)


def solution(mesh):
    spec = P(AXES, None)
    return jax.shard_map(
        on_device,
        mesh=mesh,
        in_specs=(spec,) * 6,
        out_specs=(spec,) * 4,
        check_vma=False,
    )
```

```python
import functools
import math

import jax
import jax.numpy as jnp
import ml_dtypes
import numpy as np
from jax import lax
from jax.experimental import pallas as pl
from jax.experimental.pallas import tpu as pltpu
from jax.sharding import PartitionSpec as P

AXES = ("ctx", "tp", "dp")
SEQ = 131072
ROWS = 8
LANES = 128
FIRST = 1024
SECOND = 128
HALF = FIRST // 2
QUARTER = FIRST // 4
CHUNK = 64
STEPS = QUARTER // CHUNK
BLOCK = 4 * CHUNK
ARRAYS = 4
PIECE = ARRAYS * ROWS
PAIR = 2 * ROWS
STRIDE = ROWS + 1
BACK = FIRST
FORWARD_SECOND = BACK + FIRST
INVERSE_SECOND = FORWARD_SECOND + 2 * SECOND
TABLE_WIDTH = INVERSE_SECOND + 2 * SECOND
SECOND_SCALE = 1.66569
BF16 = jnp.bfloat16
F32 = jnp.float32


@functools.cache
def make_tables():
    quarter = QUARTER * np.arange(4).reshape(1, 4, 1)
    first = (np.arange(QUARTER).reshape(STEPS, 1, CHUNK) + quarter).reshape(FIRST)
    position, second = np.arange(FIRST), np.arange(SECOND)
    product = (4 * first[:, None] + 1) * (2 * position[None, :] + 1) % (8 * FIRST)
    first_phase = 2 * np.pi * product / (8 * FIRST)
    twist_phase = 2 * np.pi * (4 * first[:, None] + 1) * (second[None, :] - SECOND // 2) / (4 * SEQ)
    forward_phase = twist_phase + np.pi / 4 * (first // QUARTER)[:, None]
    second_phase = 2 * np.pi * ((second[:, None] * second[None, :]) % SECOND) / SECOND
    scale = (SEQ * math.sqrt(SEQ) * SECOND_SCALE**3 * math.sqrt(2.0)) ** (-1 / 3)
    back = [np.cos(twist_phase) + np.sin(twist_phase), np.cos(twist_phase) - np.sin(twist_phase)]
    twist = scale * np.concatenate([np.cos(forward_phase), np.sin(forward_phase)] + back, axis=1)
    cos_second, sin_second = np.cos(second_phase), np.sin(second_phase)
    forward_second = np.block([[cos_second, sin_second], [-sin_second, cos_second]])
    inverse_second = np.block([[cos_second, -sin_second], [sin_second, cos_second]])

    columns = position.reshape(QUARTER, 4).T.reshape(FIRST)
    lowest = first_phase.reshape(STEPS // 2, 2, 4, CHUNK, FIRST)[:, :, 0].reshape(STEPS // 2, 2 * CHUNK, FIRST)
    lowest = lowest[:, :, columns]
    joined = np.zeros((FIRST, TABLE_WIDTH), ml_dtypes.bfloat16)
    joined[:HALF, :FIRST] = np.concatenate([np.cos(lowest), np.sin(lowest)], axis=1).reshape(HALF, FIRST)
    half_phase = first_phase[:, :HALF].T
    joined[:HALF, BACK : BACK + FIRST] = np.cos(half_phase - np.pi / 4)
    joined[HALF:, BACK : BACK + FIRST] = np.cos(half_phase + np.pi / 4)
    for column, table in ((FORWARD_SECOND, forward_second), (INVERSE_SECOND, inverse_second)):
        table = SECOND_SCALE * np.concatenate([table, table], axis=0)
        joined[: 4 * SECOND, column : column + 2 * SECOND] = table
    return joined, twist.astype(np.float32)


def pack_kernel(filter_hbm, first_hbm, second_hbm, gate_hbm, upstream_hbm, out_ref, local, scratch, sems):
    sources = (filter_hbm, first_hbm, second_hbm, gate_hbm, upstream_hbm)
    copies = [
        pltpu.make_async_copy(source, local.at[index], sems.at[index])
        for index, source in enumerate(sources)
    ]
    for copy in copies:
        copy.start()
    for index in range(ARRAYS):
        if index % 2 == 0:
            for copy in copies[:2] if index == 0 else copies[2:]:
                copy.wait()
        for row in range(ROWS):
            span = pl.ds(row * LANES, LANES)
            block = local[index, span, :]
            if index == ARRAYS - 1:
                block = (block.astype(F32) * local[ARRAYS, span, :].astype(F32)).astype(BF16)
            scratch[index, pl.ds(row, LANES, stride=STRIDE), :] = block.T.astype(F32)
        if index % 2:
            for channel in range(LANES):
                rows = pl.ds(channel * STRIDE, ROWS)
                pair = jnp.concatenate([scratch[index - 1, rows, :], scratch[index, rows, :]], axis=0)
                out_ref[channel, index // 2 * PAIR : (index // 2 + 1) * PAIR, :] = pair.astype(BF16)


def unpack_kernel(
    in_ref, gate_ref, upstream_ref, mixed_hbm, signal_hbm, gate_out_hbm, filter_hbm,
    scratch, halves, filter_out, sems,
):
    mirrored = lax.axis_index("ctx") >= lax.axis_size("ctx") // 2
    targets = (mixed_hbm, gate_out_hbm, signal_hbm, filter_hbm)
    copies = []
    for index in (3, 2, 0, 1):
        if index in (3, 0):
            for channel in range(LANES):
                pair = in_ref[channel, index // 2 * PAIR : (index // 2 + 1) * PAIR, :].astype(F32)
                rows = pl.ds(channel * STRIDE, ROWS)
                scratch[index // 2 * 2, rows, :] = pair[:ROWS]
                scratch[index // 2 * 2 + 1, rows, :] = pair[ROWS:]
        for row in range(ROWS):
            place = jnp.where(mirrored, ROWS - 1 - row, row)
            span = pl.ds(pl.multiple_of(place * LANES, LANES), LANES)
            block = scratch[index, pl.ds(row, LANES, stride=STRIDE), :]
            block = block.astype(BF16).T.astype(F32)
            if index == 0:
                halves[index, span, :] = (gate_ref[span, :].astype(F32) * block).astype(BF16)
            elif index == 1:
                halves[index, span, :] = (upstream_ref[span, :].astype(F32) * block).astype(BF16)
            elif index == 2:
                halves[index, span, :] = block.astype(BF16)
            else:
                filter_out[span, :] = block
        source = filter_out if index == 3 else halves.at[index]
        copies.append(pltpu.make_async_copy(source, targets[index], sems.at[index]))
        if index in (2, 1):
            for copy in copies[-2:]:
                copy.start()
    for copy in copies:
        copy.wait()


def two_pass(real, imag, table_ref, column):
    real_high, imag_high = real.astype(BF16), imag.astype(BF16)
    real_low = (real - real_high.astype(F32)).astype(BF16)
    imag_low = (imag - imag_high.astype(F32)).astype(BF16)
    joined = jnp.concatenate([real_high, imag_high, real_low, imag_low], axis=1)
    table = table_ref[: 4 * SECOND, column : column + 2 * SECOND]
    out = jnp.dot(joined, table, preferred_element_type=F32)
    return out[:, :SECOND], out[:, SECOND:]


def convolve_kernel(in_ref, table_ref, twist_ref, out_ref, rows_ref, values_ref, sum_ref, difference_ref):
    lanes = [slice(index * LANES, (index + 1) * LANES) for index in range(ARRAYS)]
    pairs = [slice(start, start + 2 * LANES) for start in range(0, ARRAYS * LANES, 2 * LANES)]

    def lay_out(pair):
        arrived = in_ref[:, pair * PAIR : (pair + 1) * PAIR, :].astype(F32)
        for index in range(2):
            part = lanes[2 * pair + index]
            rows_ref[2 * pair + index, :FIRST, :] = arrived[:, index * ROWS : (index + 1) * ROWS, :].reshape(FIRST, LANES)
            for residue in range(4):
                values_ref[residue * QUARTER : (residue + 1) * QUARTER, part] = (
                    rows_ref[2 * pair + index, pl.ds(residue, QUARTER, stride=4), :].astype(BF16)
                )

    def rows_of(step):
        return slice(step * BLOCK, (step + 1) * BLOCK)

    def first_factor(double, pair):
        rows = rows_of(double)
        p0, p1, p2, p3 = (
            jnp.dot(
                table_ref[rows, residue * QUARTER : (residue + 1) * QUARTER],
                values_ref[residue * QUARTER : (residue + 1) * QUARTER, pairs[pair]],
                preferred_element_type=F32,
            )
            for residue in range(4)
        )
        s02, d02, s13, d13 = p0 + p2, p0 - p2, p1 + p3, p1 - p3
        real, imag = slice(0, 2 * CHUNK), slice(2 * CHUNK, 4 * CHUNK)
        reals = [s02[real] + s13[real], d02[real] - d13[imag], s02[real] - s13[real], d02[real] + d13[imag]]
        imags = [s02[imag] + s13[imag], d02[imag] + d13[real], s02[imag] - s13[imag], d02[imag] - d13[real]]
        return [
            tuple(
                jnp.concatenate([value[step * CHUNK : (step + 1) * CHUNK] for value in values], axis=0)
                for values in (reals, imags)
            )
            for step in range(2)
        ]

    def second_factor(step, turned):
        real, imag = (jnp.concatenate(parts, axis=1) for parts in zip(*turned))
        cos_twist, sin_twist = twist_ref[rows_of(step), :SECOND], twist_ref[rows_of(step), SECOND : 2 * SECOND]
        return [
            two_pass(
                real[:, part] * cos_twist - imag[:, part] * sin_twist,
                real[:, part] * sin_twist + imag[:, part] * cos_twist,
                table_ref,
                FORWARD_SECOND,
            )
            for part in lanes
        ]

    def multiply(spectra):
        (fr, fi), (ar, ai), (br, bi), (mr, mi) = spectra
        products = [
            (fr * ar - fi * ai, fr * ai + fi * ar),
            (fr * br - fi * bi, fr * bi + fi * br),
            (fr * mr + fi * mi, fr * mi - fi * mr),
            (mr * br + mi * bi, mi * br - mr * bi),
        ]
        return [two_pass(real, imag, table_ref, INVERSE_SECOND) for real, imag in products]

    def store(step, results):
        sum_twist = twist_ref[rows_of(step), 2 * SECOND : 3 * SECOND]
        difference_twist = twist_ref[rows_of(step), 3 * SECOND :]
        for part, (real, imag) in zip(lanes, results):
            sum_ref[rows_of(step), part] = (real * difference_twist + imag * sum_twist).astype(BF16)
            difference_ref[rows_of(step), part] = (real * sum_twist - imag * difference_twist).astype(BF16)

    step = HALF // 4
    count = step // ROWS
    early = rows_of(STEPS - 3).stop

    def way_back(part, rows):
        columns = slice(BACK + rows.start, BACK + rows.stop)
        even = jnp.dot(
            table_ref[part * step : (part + 1) * step, columns], sum_ref[rows, :], preferred_element_type=F32
        )
        odd = jnp.dot(
            table_ref[HALF + part * step : HALF + (part + 1) * step, columns],
            difference_ref[rows, :],
            preferred_element_type=F32,
        )
        return even, odd

    turned, spectra, results, partial = {}, {}, {}, {}

    def begin(double, pair):
        for index, value in enumerate(first_factor(double, pair)):
            turned.setdefault(2 * double + index, []).append(value)

    for pair in range(2):
        lay_out(pair)
        begin(0, pair)
    for turn in range(1, STEPS + 3):
        if turn % 2 and turn + 1 < STEPS:
            for pair in range(2):
                begin((turn + 1) // 2, pair)
        if 0 <= turn - 1 < STEPS:
            spectra[turn - 1] = second_factor(turn - 1, turned.pop(turn - 1))
        if turn > STEPS:
            for part in range(2 * (turn - STEPS - 1), 2 * (turn - STEPS)):
                partial[part] = way_back(part, slice(0, early))
        if 0 <= turn - 2 < STEPS:
            results[turn - 2] = multiply(spectra.pop(turn - 2))
        if 0 <= turn - 3 < STEPS:
            store(turn - 3, results.pop(turn - 3))

    for part in range(HALF // step):
        even, odd = way_back(part, slice(early, FIRST))
        even, odd = even + partial[part][0], odd + partial[part][1]
        for result, places in (
            (even + odd, range(part * count, (part + 1) * count)),
            (even - odd, range(LANES - 1 - part * count, LANES - 1 - (part + 1) * count, -1)),
        ):
            pieces = [result[:, lane].reshape(count, ROWS, LANES) for lane in lanes]
            joined = jnp.concatenate(pieces, axis=1).astype(BF16)
            for index, place in enumerate(places):
                out_ref[place] = joined[index]


def vmem():
    return pl.BlockSpec(memory_space=pltpu.VMEM)


def hbm():
    return pl.BlockSpec(memory_space=pltpu.HBM)


def exchange(pieces):
    return lax.all_to_all(pieces, AXES, split_axis=0, concat_axis=0, tiled=True)


def on_device(signal_first, gate_first, signal_second, gate_second, upstream_second, filter_param):
    positions = ROWS * LANES
    local = jax.ShapeDtypeStruct((positions, LANES), BF16)
    pieces = jax.ShapeDtypeStruct((LANES, PIECE, LANES), BF16)
    sources = (filter_param, signal_first, signal_second, gate_second, upstream_second)
    packed = pl.pallas_call(
        pack_kernel,
        out_shape=pieces,
        in_specs=[hbm()] * 5,
        out_specs=vmem(),
        scratch_shapes=[
            pltpu.VMEM((5, positions, LANES), BF16),
            pltpu.VMEM((ARRAYS, STRIDE * LANES + PAIR, LANES), F32),
            pltpu.SemaphoreType.DMA((5,)),
        ],
        compiler_params=pltpu.CompilerParams(vmem_limit_bytes=40 * 1024 * 1024),
        cost_estimate=pl.CostEstimate(flops=20_000_000_000, bytes_accessed=2_400_000, transcendentals=0),
        name="pack",
    )(*[pltpu.with_memory_space_constraint(value, pltpu.HBM) for value in sources])
    convolved = pl.pallas_call(
        convolve_kernel,
        out_shape=pieces,
        in_specs=[vmem()] * 3,
        out_specs=vmem(),
        scratch_shapes=[pltpu.VMEM((ARRAYS, FIRST + PAIR, LANES), F32)]
        + [pltpu.VMEM((FIRST, ARRAYS * LANES), BF16)] * 3,
        compiler_params=pltpu.CompilerParams(vmem_limit_bytes=40 * 1024 * 1024),
        name="convolve",
    )(exchange(packed), *make_tables())
    return pl.pallas_call(
        unpack_kernel,
        out_shape=(local, local, local, jax.ShapeDtypeStruct((positions, LANES), F32)),
        in_specs=[vmem()] * 3,
        out_specs=(hbm(),) * 4,
        scratch_shapes=[
            pltpu.VMEM((ARRAYS, STRIDE * LANES + PAIR, LANES), F32),
            pltpu.VMEM((3, positions, LANES), BF16),
            pltpu.VMEM((positions, LANES), F32),
            pltpu.SemaphoreType.DMA((ARRAYS,)),
        ],
        compiler_params=pltpu.CompilerParams(vmem_limit_bytes=40 * 1024 * 1024),
        name="unpack",
    )(exchange(convolved), gate_first, upstream_second)


def solution(mesh):
    spec = P(AXES, None)
    return jax.shard_map(
        on_device,
        mesh=mesh,
        in_specs=(spec,) * 6,
        out_specs=(spec,) * 4,
        check_vma=False,
    )
```

```python
import functools
import math

import jax
import jax.numpy as jnp
import ml_dtypes
import numpy as np
from jax import lax
from jax.experimental import pallas as pl
from jax.experimental.pallas import tpu as pltpu
from jax.sharding import PartitionSpec as P

AXES = ("ctx", "tp", "dp")
SEQ = 131072
ROWS = 8
LANES = 128
FIRST = 1024
SECOND = 128
HALF = FIRST // 2
QUARTER = FIRST // 4
CHUNK = 64
STEPS = QUARTER // CHUNK
BLOCK = 4 * CHUNK
ARRAYS = 4
PIECE = ARRAYS * ROWS
PAIR = 2 * ROWS
STRIDE = ROWS + 1
BACK = FIRST
FORWARD_SECOND = BACK + FIRST
INVERSE_SECOND = FORWARD_SECOND + 2 * SECOND
TABLE_WIDTH = INVERSE_SECOND + 2 * SECOND
SECOND_SCALE = 1.66569
BF16 = jnp.bfloat16
F32 = jnp.float32


@functools.cache
def make_tables():
    quarter = QUARTER * np.arange(4).reshape(1, 4, 1)
    first = (np.arange(QUARTER).reshape(STEPS, 1, CHUNK) + quarter).reshape(FIRST)
    position, second = np.arange(FIRST), np.arange(SECOND)
    product = (4 * first[:, None] + 1) * (2 * position[None, :] + 1) % (8 * FIRST)
    first_phase = 2 * np.pi * product / (8 * FIRST)
    twist_phase = 2 * np.pi * (4 * first[:, None] + 1) * (second[None, :] - SECOND // 2) / (4 * SEQ)
    forward_phase = twist_phase + np.pi / 4 * (first // QUARTER)[:, None]
    second_phase = 2 * np.pi * ((second[:, None] * second[None, :]) % SECOND) / SECOND
    scale = (SEQ * math.sqrt(SEQ) * SECOND_SCALE**3 * math.sqrt(2.0)) ** (-1 / 3)
    back = [np.cos(twist_phase) + np.sin(twist_phase), np.cos(twist_phase) - np.sin(twist_phase)]
    twist = scale * np.concatenate([np.cos(forward_phase), np.sin(forward_phase)] + back, axis=1)
    cos_second, sin_second = np.cos(second_phase), np.sin(second_phase)
    forward_second = np.block([[cos_second, sin_second], [-sin_second, cos_second]])
    inverse_second = np.block([[cos_second, -sin_second], [sin_second, cos_second]])

    columns = position.reshape(QUARTER, 4).T.reshape(FIRST)
    lowest = first_phase.reshape(STEPS // 2, 2, 4, CHUNK, FIRST)[:, :, 0].reshape(STEPS // 2, 2 * CHUNK, FIRST)
    lowest = lowest[:, :, columns]
    joined = np.zeros((FIRST, TABLE_WIDTH), ml_dtypes.bfloat16)
    joined[:HALF, :FIRST] = np.concatenate([np.cos(lowest), np.sin(lowest)], axis=1).reshape(HALF, FIRST)
    half_phase = first_phase[:, :HALF].T
    joined[:HALF, BACK : BACK + FIRST] = np.cos(half_phase - np.pi / 4)
    joined[HALF:, BACK : BACK + FIRST] = np.cos(half_phase + np.pi / 4)
    for column, table in ((FORWARD_SECOND, forward_second), (INVERSE_SECOND, inverse_second)):
        table = SECOND_SCALE * np.concatenate([table, table], axis=0)
        joined[: 4 * SECOND, column : column + 2 * SECOND] = table
    return joined, twist.astype(np.float32)


def pack_kernel(filter_hbm, first_hbm, second_hbm, gate_hbm, upstream_hbm, out_ref, local, scratch, sems):
    sources = (filter_hbm, first_hbm, second_hbm, gate_hbm, upstream_hbm)
    copies = [
        pltpu.make_async_copy(source, local.at[index], sems.at[index])
        for index, source in enumerate(sources)
    ]
    for copy in copies:
        copy.start()
    for index in range(ARRAYS):
        if index % 2 == 0:
            for copy in copies[:2] if index == 0 else copies[2:]:
                copy.wait()
        for row in range(ROWS):
            span = pl.ds(row * LANES, LANES)
            block = local[index, span, :]
            if index == ARRAYS - 1:
                block = (block.astype(F32) * local[ARRAYS, span, :].astype(F32)).astype(BF16)
            scratch[index, pl.ds(row, LANES, stride=STRIDE), :] = block.T.astype(F32)
        if index % 2:
            for channel in range(LANES):
                rows = pl.ds(channel * STRIDE, ROWS)
                pair = jnp.concatenate([scratch[index - 1, rows, :], scratch[index, rows, :]], axis=0)
                out_ref[channel, index // 2 * PAIR : (index // 2 + 1) * PAIR, :] = pair.astype(BF16)


def unpack_kernel(
    in_ref, gate_ref, upstream_ref, mixed_hbm, signal_hbm, gate_out_hbm, filter_hbm,
    scratch, halves, filter_out, sems,
):
    mirrored = lax.axis_index("ctx") >= lax.axis_size("ctx") // 2
    targets = (mixed_hbm, gate_out_hbm, signal_hbm, filter_hbm)
    copies = []
    for index in (3, 2, 0, 1):
        if index in (3, 0):
            for channel in range(LANES):
                pair = in_ref[channel, index // 2 * PAIR : (index // 2 + 1) * PAIR, :].astype(F32)
                rows = pl.ds(channel * STRIDE, ROWS)
                scratch[index // 2 * 2, rows, :] = pair[:ROWS]
                scratch[index // 2 * 2 + 1, rows, :] = pair[ROWS:]
        for row in range(ROWS):
            place = jnp.where(mirrored, ROWS - 1 - row, row)
            span = pl.ds(pl.multiple_of(place * LANES, LANES), LANES)
            block = scratch[index, pl.ds(row, LANES, stride=STRIDE), :]
            block = block.astype(BF16).T.astype(F32)
            if index == 0:
                halves[index, span, :] = (gate_ref[span, :].astype(F32) * block).astype(BF16)
            elif index == 1:
                halves[index, span, :] = (upstream_ref[span, :].astype(F32) * block).astype(BF16)
            elif index == 2:
                halves[index, span, :] = block.astype(BF16)
            else:
                filter_out[span, :] = block
        source = filter_out if index == 3 else halves.at[index]
        copies.append(pltpu.make_async_copy(source, targets[index], sems.at[index]))
        if index in (2, 1):
            for copy in copies[-2:]:
                copy.start()
    for copy in copies:
        copy.wait()


def two_pass(real, imag, table_ref, column):
    real_high, imag_high = real.astype(BF16), imag.astype(BF16)
    real_low = (real - real_high.astype(F32)).astype(BF16)
    imag_low = (imag - imag_high.astype(F32)).astype(BF16)
    joined = jnp.concatenate([real_high, imag_high, real_low, imag_low], axis=1)
    table = table_ref[: 4 * SECOND, column : column + 2 * SECOND]
    out = jnp.dot(joined, table, preferred_element_type=F32)
    return out[:, :SECOND], out[:, SECOND:]


def convolve_kernel(in_ref, table_ref, twist_ref, out_ref, rows_ref, values_ref, sum_ref, difference_ref):
    lanes = [slice(index * LANES, (index + 1) * LANES) for index in range(ARRAYS)]
    pairs = [slice(start, start + 2 * LANES) for start in range(0, ARRAYS * LANES, 2 * LANES)]

    def lay_out(pair):
        arrived = in_ref[:, pair * PAIR : (pair + 1) * PAIR, :].astype(F32)
        for index in range(2):
            part = lanes[2 * pair + index]
            rows_ref[2 * pair + index, :FIRST, :] = arrived[:, index * ROWS : (index + 1) * ROWS, :].reshape(FIRST, LANES)
            for residue in range(4):
                values_ref[residue * QUARTER : (residue + 1) * QUARTER, part] = (
                    rows_ref[2 * pair + index, pl.ds(residue, QUARTER, stride=4), :].astype(BF16)
                )

    def rows_of(step):
        return slice(step * BLOCK, (step + 1) * BLOCK)

    def first_factor(double, pair):
        rows = rows_of(double)
        p0, p1, p2, p3 = (
            jnp.dot(
                table_ref[rows, residue * QUARTER : (residue + 1) * QUARTER],
                values_ref[residue * QUARTER : (residue + 1) * QUARTER, pairs[pair]],
                preferred_element_type=F32,
            )
            for residue in range(4)
        )
        s02, d02, s13, d13 = p0 + p2, p0 - p2, p1 + p3, p1 - p3
        real, imag = slice(0, 2 * CHUNK), slice(2 * CHUNK, 4 * CHUNK)
        reals = [s02[real] + s13[real], d02[real] - d13[imag], s02[real] - s13[real], d02[real] + d13[imag]]
        imags = [s02[imag] + s13[imag], d02[imag] + d13[real], s02[imag] - s13[imag], d02[imag] - d13[real]]
        return [
            tuple(
                jnp.concatenate([value[step * CHUNK : (step + 1) * CHUNK] for value in values], axis=0)
                for values in (reals, imags)
            )
            for step in range(2)
        ]

    def second_factor(step, turned):
        real, imag = (jnp.concatenate(parts, axis=1) for parts in zip(*turned))
        cos_twist, sin_twist = twist_ref[rows_of(step), :SECOND], twist_ref[rows_of(step), SECOND : 2 * SECOND]
        return [
            two_pass(
                real[:, part] * cos_twist - imag[:, part] * sin_twist,
                real[:, part] * sin_twist + imag[:, part] * cos_twist,
                table_ref,
                FORWARD_SECOND,
            )
            for part in lanes
        ]

    def multiply(spectra):
        (fr, fi), (ar, ai), (br, bi), (mr, mi) = spectra
        products = [
            (fr * ar - fi * ai, fr * ai + fi * ar),
            (fr * br - fi * bi, fr * bi + fi * br),
            (fr * mr + fi * mi, fr * mi - fi * mr),
            (mr * br + mi * bi, mi * br - mr * bi),
        ]
        return [two_pass(real, imag, table_ref, INVERSE_SECOND) for real, imag in products]

    def store(step, results):
        sum_twist = twist_ref[rows_of(step), 2 * SECOND : 3 * SECOND]
        difference_twist = twist_ref[rows_of(step), 3 * SECOND :]
        for part, (real, imag) in zip(lanes, results):
            sum_ref[rows_of(step), part] = (real * difference_twist + imag * sum_twist).astype(BF16)
            difference_ref[rows_of(step), part] = (real * sum_twist - imag * difference_twist).astype(BF16)

    step = HALF // 4
    count = step // ROWS
    early = rows_of(STEPS - 2).stop

    def way_back(part, rows):
        columns = slice(BACK + rows.start, BACK + rows.stop)
        even = jnp.dot(
            table_ref[part * step : (part + 1) * step, columns], sum_ref[rows, :], preferred_element_type=F32
        )
        odd = jnp.dot(
            table_ref[HALF + part * step : HALF + (part + 1) * step, columns],
            difference_ref[rows, :],
            preferred_element_type=F32,
        )
        return even, odd

    turned, spectra, results, partial = {}, {}, {}, {}

    def begin(double, pair):
        for index, value in enumerate(first_factor(double, pair)):
            turned.setdefault(2 * double + index, []).append(value)

    for pair in range(2):
        lay_out(pair)
        begin(0, pair)
    for turn in range(1, STEPS + 3):
        if 0 <= turn - 3 < STEPS:
            store(turn - 3, results.pop(turn - 3))
        if turn > STEPS:
            for part in range(2 * (turn - STEPS - 1), 2 * (turn - STEPS)):
                partial[part] = way_back(part, slice(0, early))
        if 0 <= turn - 2 < STEPS:
            results[turn - 2] = multiply(spectra.pop(turn - 2))
        if 0 <= turn - 1 < STEPS:
            spectra[turn - 1] = second_factor(turn - 1, turned.pop(turn - 1))
        if turn % 2 and turn + 1 < STEPS:
            for pair in range(2):
                begin((turn + 1) // 2, pair)

    for part in range(HALF // step):
        even, odd = way_back(part, slice(early, FIRST))
        even, odd = even + partial[part][0], odd + partial[part][1]
        for result, places in (
            (even + odd, range(part * count, (part + 1) * count)),
            (even - odd, range(LANES - 1 - part * count, LANES - 1 - (part + 1) * count, -1)),
        ):
            pieces = [result[:, lane].reshape(count, ROWS, LANES) for lane in lanes]
            joined = jnp.concatenate(pieces, axis=1).astype(BF16)
            for index, place in enumerate(places):
                out_ref[place] = joined[index]


def vmem():
    return pl.BlockSpec(memory_space=pltpu.VMEM)


def hbm():
    return pl.BlockSpec(memory_space=pltpu.HBM)


def exchange(pieces):
    return lax.all_to_all(pieces, AXES, split_axis=0, concat_axis=0, tiled=True)


def on_device(signal_first, gate_first, signal_second, gate_second, upstream_second, filter_param):
    positions = ROWS * LANES
    local = jax.ShapeDtypeStruct((positions, LANES), BF16)
    pieces = jax.ShapeDtypeStruct((LANES, PIECE, LANES), BF16)
    sources = (filter_param, signal_first, signal_second, gate_second, upstream_second)
    packed = pl.pallas_call(
        pack_kernel,
        out_shape=pieces,
        in_specs=[hbm()] * 5,
        out_specs=vmem(),
        scratch_shapes=[
            pltpu.VMEM((5, positions, LANES), BF16),
            pltpu.VMEM((ARRAYS, STRIDE * LANES + PAIR, LANES), F32),
            pltpu.SemaphoreType.DMA((5,)),
        ],
        compiler_params=pltpu.CompilerParams(vmem_limit_bytes=40 * 1024 * 1024),
        cost_estimate=pl.CostEstimate(flops=20_000_000_000, bytes_accessed=2_400_000, transcendentals=0),
        name="pack",
    )(*[pltpu.with_memory_space_constraint(value, pltpu.HBM) for value in sources])
    convolved = pl.pallas_call(
        convolve_kernel,
        out_shape=pieces,
        in_specs=[vmem()] * 3,
        out_specs=vmem(),
        scratch_shapes=[pltpu.VMEM((ARRAYS, FIRST + PAIR, LANES), F32)]
        + [pltpu.VMEM((FIRST, ARRAYS * LANES), BF16)] * 3,
        compiler_params=pltpu.CompilerParams(vmem_limit_bytes=40 * 1024 * 1024),
        name="convolve",
    )(exchange(packed), *make_tables())
    return pl.pallas_call(
        unpack_kernel,
        out_shape=(local, local, local, jax.ShapeDtypeStruct((positions, LANES), F32)),
        in_specs=[vmem()] * 3,
        out_specs=(hbm(),) * 4,
        scratch_shapes=[
            pltpu.VMEM((ARRAYS, STRIDE * LANES + PAIR, LANES), F32),
            pltpu.VMEM((3, positions, LANES), BF16),
            pltpu.VMEM((positions, LANES), F32),
            pltpu.SemaphoreType.DMA((ARRAYS,)),
        ],
        compiler_params=pltpu.CompilerParams(vmem_limit_bytes=40 * 1024 * 1024),
        name="unpack",
    )(exchange(convolved), gate_first, upstream_second)


def solution(mesh):
    spec = P(AXES, None)
    return jax.shard_map(
        on_device,
        mesh=mesh,
        in_specs=(spec,) * 6,
        out_specs=(spec,) * 4,
        check_vma=False,
    )
```

```python
import functools
import math

import jax
import jax.numpy as jnp
import ml_dtypes
import numpy as np
from jax import lax
from jax.experimental import pallas as pl
from jax.experimental.pallas import tpu as pltpu
from jax.sharding import PartitionSpec as P

AXES = ("ctx", "tp", "dp")
SEQ = 131072
ROWS = 8
LANES = 128
FIRST = 1024
SECOND = 128
HALF = FIRST // 2
QUARTER = FIRST // 4
CHUNK = 64
STEPS = QUARTER // CHUNK
BLOCK = 4 * CHUNK
ARRAYS = 4
PIECE = ARRAYS * ROWS
PAIR = 2 * ROWS
STRIDE = ROWS + 1
BACK = FIRST
FORWARD_SECOND = BACK + FIRST
INVERSE_SECOND = FORWARD_SECOND + 2 * SECOND
TABLE_WIDTH = INVERSE_SECOND + 2 * SECOND
SECOND_SCALE = 1.66569
BF16 = jnp.bfloat16
F32 = jnp.float32


@functools.cache
def make_tables():
    quarter = QUARTER * np.arange(4).reshape(1, 4, 1)
    first = (np.arange(QUARTER).reshape(STEPS, 1, CHUNK) + quarter).reshape(FIRST)
    position, second = np.arange(FIRST), np.arange(SECOND)
    product = (4 * first[:, None] + 1) * (2 * position[None, :] + 1) % (8 * FIRST)
    first_phase = 2 * np.pi * product / (8 * FIRST)
    twist_phase = 2 * np.pi * (4 * first[:, None] + 1) * (second[None, :] - SECOND // 2) / (4 * SEQ)
    forward_phase = twist_phase + np.pi / 4 * (first // QUARTER)[:, None]
    second_phase = 2 * np.pi * ((second[:, None] * second[None, :]) % SECOND) / SECOND
    scale = (SEQ * math.sqrt(SEQ) * SECOND_SCALE**3 * math.sqrt(2.0)) ** (-1 / 3)
    back = [np.cos(twist_phase) + np.sin(twist_phase), np.cos(twist_phase) - np.sin(twist_phase)]
    twist = scale * np.concatenate([np.cos(forward_phase), np.sin(forward_phase)] + back, axis=1)
    cos_second, sin_second = np.cos(second_phase), np.sin(second_phase)
    forward_second = np.block([[cos_second, sin_second], [-sin_second, cos_second]])
    inverse_second = np.block([[cos_second, -sin_second], [sin_second, cos_second]])

    columns = position.reshape(QUARTER, 4).T.reshape(FIRST)
    lowest = first_phase.reshape(STEPS // 2, 2, 4, CHUNK, FIRST)[:, :, 0].reshape(STEPS // 2, 2 * CHUNK, FIRST)
    lowest = lowest[:, :, columns]
    joined = np.zeros((FIRST, TABLE_WIDTH), ml_dtypes.bfloat16)
    joined[:HALF, :FIRST] = np.concatenate([np.cos(lowest), np.sin(lowest)], axis=1).reshape(HALF, FIRST)
    half_phase = first_phase[:, :HALF].T
    joined[:HALF, BACK : BACK + FIRST] = np.cos(half_phase - np.pi / 4)
    joined[HALF:, BACK : BACK + FIRST] = np.cos(half_phase + np.pi / 4)
    for column, table in ((FORWARD_SECOND, forward_second), (INVERSE_SECOND, inverse_second)):
        table = SECOND_SCALE * np.concatenate([table, table], axis=0)
        joined[: 4 * SECOND, column : column + 2 * SECOND] = table
    return joined, twist.astype(np.float32)


def pack_kernel(filter_hbm, first_hbm, second_hbm, gate_hbm, upstream_hbm, out_ref, local, scratch, sems):
    sources = (filter_hbm, first_hbm, second_hbm, gate_hbm, upstream_hbm)
    copies = [
        pltpu.make_async_copy(source, local.at[index], sems.at[index])
        for index, source in enumerate(sources)
    ]
    for copy in copies:
        copy.start()
    for index in range(ARRAYS):
        if index % 2 == 0:
            for copy in copies[:2] if index == 0 else copies[2:]:
                copy.wait()
        for row in range(ROWS):
            span = pl.ds(row * LANES, LANES)
            block = local[index, span, :]
            if index == ARRAYS - 1:
                block = (block.astype(F32) * local[ARRAYS, span, :].astype(F32)).astype(BF16)
            scratch[index, pl.ds(row, LANES, stride=STRIDE), :] = block.T.astype(F32)
        if index % 2:
            for channel in range(LANES):
                rows = pl.ds(channel * STRIDE, ROWS)
                pair = jnp.concatenate([scratch[index - 1, rows, :], scratch[index, rows, :]], axis=0)
                out_ref[channel, index // 2 * PAIR : (index // 2 + 1) * PAIR, :] = pair.astype(BF16)


def unpack_kernel(
    in_ref, gate_ref, upstream_ref, mixed_hbm, signal_hbm, gate_out_hbm, filter_hbm,
    scratch, halves, filter_out, sems,
):
    mirrored = lax.axis_index("ctx") >= lax.axis_size("ctx") // 2
    targets = (mixed_hbm, gate_out_hbm, signal_hbm, filter_hbm)
    copies = []
    for index in (3, 2, 0, 1):
        if index in (3, 0):
            for channel in range(LANES):
                pair = in_ref[channel, index // 2 * PAIR : (index // 2 + 1) * PAIR, :].astype(F32)
                rows = pl.ds(channel * STRIDE, ROWS)
                scratch[index // 2 * 2, rows, :] = pair[:ROWS]
                scratch[index // 2 * 2 + 1, rows, :] = pair[ROWS:]
        for row in range(ROWS):
            place = jnp.where(mirrored, ROWS - 1 - row, row)
            span = pl.ds(pl.multiple_of(place * LANES, LANES), LANES)
            block = scratch[index, pl.ds(row, LANES, stride=STRIDE), :]
            block = block.astype(BF16).T.astype(F32)
            if index == 0:
                halves[index, span, :] = (gate_ref[span, :].astype(F32) * block).astype(BF16)
            elif index == 1:
                halves[index, span, :] = (upstream_ref[span, :].astype(F32) * block).astype(BF16)
            elif index == 2:
                halves[index, span, :] = block.astype(BF16)
            else:
                filter_out[span, :] = block
        source = filter_out if index == 3 else halves.at[index]
        copies.append(pltpu.make_async_copy(source, targets[index], sems.at[index]))
        if index in (2, 1):
            for copy in copies[-2:]:
                copy.start()
    for copy in copies:
        copy.wait()


def two_pass(real, imag, table_ref, column):
    real_high, imag_high = real.astype(BF16), imag.astype(BF16)
    real_low = (real - real_high.astype(F32)).astype(BF16)
    imag_low = (imag - imag_high.astype(F32)).astype(BF16)
    joined = jnp.concatenate([real_high, imag_high, real_low, imag_low], axis=1)
    table = table_ref[: 4 * SECOND, column : column + 2 * SECOND]
    out = jnp.dot(joined, table, preferred_element_type=F32)
    return out[:, :SECOND], out[:, SECOND:]


def convolve_kernel(in_ref, table_ref, twist_ref, out_ref, rows_ref, values_ref, sum_ref, difference_ref):
    lanes = [slice(index * LANES, (index + 1) * LANES) for index in range(ARRAYS)]
    pairs = [slice(start, start + 2 * LANES) for start in range(0, ARRAYS * LANES, 2 * LANES)]

    def lay_out(pair):
        arrived = in_ref[:, pair * PAIR : (pair + 1) * PAIR, :].astype(F32)
        for index in range(2):
            part = lanes[2 * pair + index]
            rows_ref[2 * pair + index, :FIRST, :] = arrived[:, index * ROWS : (index + 1) * ROWS, :].reshape(FIRST, LANES)
            for residue in range(4):
                values_ref[residue * QUARTER : (residue + 1) * QUARTER, part] = (
                    rows_ref[2 * pair + index, pl.ds(residue, QUARTER, stride=4), :].astype(BF16)
                )

    def rows_of(step):
        return slice(step * BLOCK, (step + 1) * BLOCK)

    def first_factor(double, pair):
        rows = rows_of(double)
        p0, p1, p2, p3 = (
            jnp.dot(
                table_ref[rows, residue * QUARTER : (residue + 1) * QUARTER],
                values_ref[residue * QUARTER : (residue + 1) * QUARTER, pairs[pair]],
                preferred_element_type=F32,
            )
            for residue in range(4)
        )
        s02, d02, s13, d13 = p0 + p2, p0 - p2, p1 + p3, p1 - p3
        real, imag = slice(0, 2 * CHUNK), slice(2 * CHUNK, 4 * CHUNK)
        reals = [s02[real] + s13[real], d02[real] - d13[imag], s02[real] - s13[real], d02[real] + d13[imag]]
        imags = [s02[imag] + s13[imag], d02[imag] + d13[real], s02[imag] - s13[imag], d02[imag] - d13[real]]
        return [
            tuple(
                jnp.concatenate([value[step * CHUNK : (step + 1) * CHUNK] for value in values], axis=0)
                for values in (reals, imags)
            )
            for step in range(2)
        ]

    def second_factor(step, turned, index):
        real, imag = turned[index // 2]
        part = lanes[index % 2]
        cos_twist, sin_twist = twist_ref[rows_of(step), :SECOND], twist_ref[rows_of(step), SECOND : 2 * SECOND]
        return two_pass(
            real[:, part] * cos_twist - imag[:, part] * sin_twist,
            real[:, part] * sin_twist + imag[:, part] * cos_twist,
            table_ref,
            FORWARD_SECOND,
        )

    def multiply(spectra, index):
        (fr, fi), (ar, ai), (br, bi), (mr, mi) = spectra
        if index == 0:
            real, imag = fr * ar - fi * ai, fr * ai + fi * ar
        elif index == 1:
            real, imag = fr * br - fi * bi, fr * bi + fi * br
        elif index == 2:
            real, imag = fr * mr + fi * mi, fr * mi - fi * mr
        else:
            real, imag = mr * br + mi * bi, mi * br - mr * bi
        return two_pass(real, imag, table_ref, INVERSE_SECOND)

    def store(step, results):
        sum_twist = twist_ref[rows_of(step), 2 * SECOND : 3 * SECOND]
        difference_twist = twist_ref[rows_of(step), 3 * SECOND :]
        for part, (real, imag) in zip(lanes, results):
            sum_ref[rows_of(step), part] = (real * difference_twist + imag * sum_twist).astype(BF16)
            difference_ref[rows_of(step), part] = (real * sum_twist - imag * difference_twist).astype(BF16)

    step = HALF // 4
    count = step // ROWS
    early = rows_of(STEPS - 2).stop

    def way_back(part, rows):
        columns = slice(BACK + rows.start, BACK + rows.stop)
        even = jnp.dot(
            table_ref[part * step : (part + 1) * step, columns], sum_ref[rows, :], preferred_element_type=F32
        )
        odd = jnp.dot(
            table_ref[HALF + part * step : HALF + (part + 1) * step, columns],
            difference_ref[rows, :],
            preferred_element_type=F32,
        )
        return even, odd

    turned, spectra, results, partial = {}, {}, {}, {}

    def begin(double, pair):
        for index, value in enumerate(first_factor(double, pair)):
            turned.setdefault(2 * double + index, []).append(value)

    for pair in range(2):
        lay_out(pair)
        begin(0, pair)
    for turn in range(1, STEPS + 3):
        if 0 <= turn - 3 < STEPS:
            store(turn - 3, results.pop(turn - 3))
        if turn > STEPS:
            for part in range(2 * (turn - STEPS - 1), 2 * (turn - STEPS)):
                partial[part] = way_back(part, slice(0, early))
        for index in range(ARRAYS):
            if 0 <= turn - 2 < STEPS:
                results.setdefault(turn - 2, []).append(multiply(spectra[turn - 2], index))
            if 0 <= turn - 1 < STEPS:
                spectra.setdefault(turn - 1, []).append(second_factor(turn - 1, turned[turn - 1], index))
            if turn % 2 and turn + 1 < STEPS and index % 2:
                begin((turn + 1) // 2, index // 2)

    for part in range(HALF // step):
        even, odd = way_back(part, slice(early, FIRST))
        even, odd = even + partial[part][0], odd + partial[part][1]
        for result, places in (
            (even + odd, range(part * count, (part + 1) * count)),
            (even - odd, range(LANES - 1 - part * count, LANES - 1 - (part + 1) * count, -1)),
        ):
            pieces = [result[:, lane].reshape(count, ROWS, LANES) for lane in lanes]
            joined = jnp.concatenate(pieces, axis=1).astype(BF16)
            for index, place in enumerate(places):
                out_ref[place] = joined[index]


def vmem():
    return pl.BlockSpec(memory_space=pltpu.VMEM)


def hbm():
    return pl.BlockSpec(memory_space=pltpu.HBM)


def exchange(pieces):
    return lax.all_to_all(pieces, AXES, split_axis=0, concat_axis=0, tiled=True)


def on_device(signal_first, gate_first, signal_second, gate_second, upstream_second, filter_param):
    positions = ROWS * LANES
    local = jax.ShapeDtypeStruct((positions, LANES), BF16)
    pieces = jax.ShapeDtypeStruct((LANES, PIECE, LANES), BF16)
    sources = (filter_param, signal_first, signal_second, gate_second, upstream_second)
    packed = pl.pallas_call(
        pack_kernel,
        out_shape=pieces,
        in_specs=[hbm()] * 5,
        out_specs=vmem(),
        scratch_shapes=[
            pltpu.VMEM((5, positions, LANES), BF16),
            pltpu.VMEM((ARRAYS, STRIDE * LANES + PAIR, LANES), F32),
            pltpu.SemaphoreType.DMA((5,)),
        ],
        compiler_params=pltpu.CompilerParams(vmem_limit_bytes=40 * 1024 * 1024),
        cost_estimate=pl.CostEstimate(flops=20_000_000_000, bytes_accessed=2_400_000, transcendentals=0),
        name="pack",
    )(*[pltpu.with_memory_space_constraint(value, pltpu.HBM) for value in sources])
    convolved = pl.pallas_call(
        convolve_kernel,
        out_shape=pieces,
        in_specs=[vmem()] * 3,
        out_specs=vmem(),
        scratch_shapes=[pltpu.VMEM((ARRAYS, FIRST + PAIR, LANES), F32)]
        + [pltpu.VMEM((FIRST, ARRAYS * LANES), BF16)] * 3,
        compiler_params=pltpu.CompilerParams(vmem_limit_bytes=40 * 1024 * 1024),
        name="convolve",
    )(exchange(packed), *make_tables())
    return pl.pallas_call(
        unpack_kernel,
        out_shape=(local, local, local, jax.ShapeDtypeStruct((positions, LANES), F32)),
        in_specs=[vmem()] * 3,
        out_specs=(hbm(),) * 4,
        scratch_shapes=[
            pltpu.VMEM((ARRAYS, STRIDE * LANES + PAIR, LANES), F32),
            pltpu.VMEM((3, positions, LANES), BF16),
            pltpu.VMEM((positions, LANES), F32),
            pltpu.SemaphoreType.DMA((ARRAYS,)),
        ],
        compiler_params=pltpu.CompilerParams(vmem_limit_bytes=40 * 1024 * 1024),
        name="unpack",
    )(exchange(convolved), gate_first, upstream_second)


def solution(mesh):
    spec = P(AXES, None)
    return jax.shard_map(
        on_device,
        mesh=mesh,
        in_specs=(spec,) * 6,
        out_specs=(spec,) * 4,
        check_vma=False,
    )
```

```python
import functools
import math

import jax
import jax.numpy as jnp
import ml_dtypes
import numpy as np
from jax import lax
from jax.experimental import pallas as pl
from jax.experimental.pallas import tpu as pltpu
from jax.sharding import PartitionSpec as P

AXES = ("ctx", "tp", "dp")
SEQ = 131072
ROWS = 8
LANES = 128
FIRST = 1024
SECOND = 128
HALF = FIRST // 2
QUARTER = FIRST // 4
CHUNK = 64
STEPS = QUARTER // CHUNK
BLOCK = 4 * CHUNK
ARRAYS = 4
PIECE = ARRAYS * ROWS
PAIR = 2 * ROWS
STRIDE = ROWS + 1
BACK = FIRST
FORWARD_SECOND = BACK + FIRST
INVERSE_SECOND = FORWARD_SECOND + 2 * SECOND
TABLE_WIDTH = INVERSE_SECOND + 2 * SECOND
SECOND_SCALE = 1.66569
BF16 = jnp.bfloat16
F32 = jnp.float32


@functools.cache
def make_tables():
    quarter = QUARTER * np.arange(4).reshape(1, 4, 1)
    first = (np.arange(QUARTER).reshape(STEPS, 1, CHUNK) + quarter).reshape(FIRST)
    position, second = np.arange(FIRST), np.arange(SECOND)
    product = (4 * first[:, None] + 1) * (2 * position[None, :] + 1) % (8 * FIRST)
    first_phase = 2 * np.pi * product / (8 * FIRST)
    twist_phase = 2 * np.pi * (4 * first[:, None] + 1) * (second[None, :] - SECOND // 2) / (4 * SEQ)
    forward_phase = twist_phase + np.pi / 4 * (first // QUARTER)[:, None]
    second_phase = 2 * np.pi * ((second[:, None] * second[None, :]) % SECOND) / SECOND
    scale = (SEQ * math.sqrt(SEQ) * SECOND_SCALE**3 * math.sqrt(2.0)) ** (-1 / 3)
    back = [np.cos(twist_phase) + np.sin(twist_phase), np.cos(twist_phase) - np.sin(twist_phase)]
    twist = scale * np.concatenate([np.cos(forward_phase), np.sin(forward_phase)] + back, axis=1)
    cos_second, sin_second = np.cos(second_phase), np.sin(second_phase)
    forward_second = np.block([[cos_second, sin_second], [-sin_second, cos_second]])
    inverse_second = np.block([[cos_second, -sin_second], [sin_second, cos_second]])

    columns = position.reshape(QUARTER, 4).T.reshape(FIRST)
    lowest = first_phase.reshape(STEPS // 2, 2, 4, CHUNK, FIRST)[:, :, 0].reshape(STEPS // 2, 2 * CHUNK, FIRST)
    lowest = lowest[:, :, columns]
    joined = np.zeros((FIRST, TABLE_WIDTH), ml_dtypes.bfloat16)
    joined[:HALF, :FIRST] = np.concatenate([np.cos(lowest), np.sin(lowest)], axis=1).reshape(HALF, FIRST)
    half_phase = first_phase[:, :HALF].T
    joined[:HALF, BACK : BACK + FIRST] = np.cos(half_phase - np.pi / 4)
    joined[HALF:, BACK : BACK + FIRST] = np.cos(half_phase + np.pi / 4)
    for column, table in ((FORWARD_SECOND, forward_second), (INVERSE_SECOND, inverse_second)):
        table = SECOND_SCALE * np.concatenate([table, table], axis=0)
        joined[: 4 * SECOND, column : column + 2 * SECOND] = table
    return joined, twist.astype(np.float32)


def pack_kernel(filter_hbm, first_hbm, second_hbm, gate_hbm, upstream_hbm, out_ref, local, scratch, sems):
    sources = (filter_hbm, first_hbm, second_hbm, gate_hbm, upstream_hbm)
    copies = [
        pltpu.make_async_copy(source, local.at[index], sems.at[index])
        for index, source in enumerate(sources)
    ]
    for copy in copies:
        copy.start()
    for index in range(ARRAYS):
        if index % 2 == 0:
            for copy in copies[:2] if index == 0 else copies[2:]:
                copy.wait()
        for row in range(ROWS):
            span = pl.ds(row * LANES, LANES)
            block = local[index, span, :]
            if index == ARRAYS - 1:
                block = (block.astype(F32) * local[ARRAYS, span, :].astype(F32)).astype(BF16)
            scratch[index, pl.ds(row, LANES, stride=STRIDE), :] = block.T.astype(F32)
        if index % 2:
            for channel in range(LANES):
                rows = pl.ds(channel * STRIDE, ROWS)
                pair = jnp.concatenate([scratch[index - 1, rows, :], scratch[index, rows, :]], axis=0)
                out_ref[channel, index // 2 * PAIR : (index // 2 + 1) * PAIR, :] = pair.astype(BF16)


def unpack_kernel(
    in_ref, gate_ref, upstream_ref, mixed_hbm, signal_hbm, gate_out_hbm, filter_hbm,
    scratch, halves, filter_out, sems,
):
    mirrored = lax.axis_index("ctx") >= lax.axis_size("ctx") // 2
    targets = (mixed_hbm, gate_out_hbm, signal_hbm, filter_hbm)
    copies = []
    for index in (3, 2, 0, 1):
        if index in (3, 0):
            for channel in range(LANES):
                pair = in_ref[channel, index // 2 * PAIR : (index // 2 + 1) * PAIR, :].astype(F32)
                rows = pl.ds(channel * STRIDE, ROWS)
                scratch[index // 2 * 2, rows, :] = pair[:ROWS]
                scratch[index // 2 * 2 + 1, rows, :] = pair[ROWS:]
        for row in range(ROWS):
            place = jnp.where(mirrored, ROWS - 1 - row, row)
            span = pl.ds(pl.multiple_of(place * LANES, LANES), LANES)
            block = scratch[index, pl.ds(row, LANES, stride=STRIDE), :]
            block = block.astype(BF16).T.astype(F32)
            if index == 0:
                halves[index, span, :] = (gate_ref[span, :].astype(F32) * block).astype(BF16)
            elif index == 1:
                halves[index, span, :] = (upstream_ref[span, :].astype(F32) * block).astype(BF16)
            elif index == 2:
                halves[index, span, :] = block.astype(BF16)
            else:
                filter_out[span, :] = block
        source = filter_out if index == 3 else halves.at[index]
        copies.append(pltpu.make_async_copy(source, targets[index], sems.at[index]))
        if index in (2, 1):
            for copy in copies[-2:]:
                copy.start()
    for copy in copies:
        copy.wait()


def two_pass(real, imag, table_ref, column):
    real_high, imag_high = real.astype(BF16), imag.astype(BF16)
    real_low = (real - real_high.astype(F32)).astype(BF16)
    imag_low = (imag - imag_high.astype(F32)).astype(BF16)
    joined = jnp.concatenate([real_high, imag_high, real_low, imag_low], axis=1)
    table = table_ref[: 4 * SECOND, column : column + 2 * SECOND]
    out = jnp.dot(joined, table, preferred_element_type=F32)
    return out[:, :SECOND], out[:, SECOND:]


def convolve_kernel(in_ref, table_ref, twist_ref, out_ref, rows_ref, values_ref, sum_ref, difference_ref):
    lanes = [slice(index * LANES, (index + 1) * LANES) for index in range(ARRAYS)]
    pairs = [slice(start, start + 2 * LANES) for start in range(0, ARRAYS * LANES, 2 * LANES)]

    def lay_out(pair):
        arrived = in_ref[:, pair * PAIR : (pair + 1) * PAIR, :].astype(F32)
        for index in range(2):
            part = lanes[2 * pair + index]
            rows_ref[2 * pair + index, :FIRST, :] = arrived[:, index * ROWS : (index + 1) * ROWS, :].reshape(FIRST, LANES)
            for residue in range(4):
                values_ref[residue * QUARTER : (residue + 1) * QUARTER, part] = (
                    rows_ref[2 * pair + index, pl.ds(residue, QUARTER, stride=4), :].astype(BF16)
                )

    def rows_of(step):
        return slice(step * BLOCK, (step + 1) * BLOCK)

    def first_factor(double, pair):
        rows = rows_of(double)
        p0, p1, p2, p3 = (
            jnp.dot(
                table_ref[rows, residue * QUARTER : (residue + 1) * QUARTER],
                values_ref[residue * QUARTER : (residue + 1) * QUARTER, pairs[pair]],
                preferred_element_type=F32,
            )
            for residue in range(4)
        )
        s02, d02, s13, d13 = p0 + p2, p0 - p2, p1 + p3, p1 - p3
        real, imag = slice(0, 2 * CHUNK), slice(2 * CHUNK, 4 * CHUNK)
        reals = [s02[real] + s13[real], d02[real] - d13[imag], s02[real] - s13[real], d02[real] + d13[imag]]
        imags = [s02[imag] + s13[imag], d02[imag] + d13[real], s02[imag] - s13[imag], d02[imag] - d13[real]]
        return [
            tuple(
                jnp.concatenate([value[step * CHUNK : (step + 1) * CHUNK] for value in values], axis=0)
                for values in (reals, imags)
            )
            for step in range(2)
        ]

    def second_factor(step, turned):
        real, imag = (jnp.concatenate(parts, axis=1) for parts in zip(*turned))
        cos_twist, sin_twist = twist_ref[rows_of(step), :SECOND], twist_ref[rows_of(step), SECOND : 2 * SECOND]
        return [
            two_pass(
                real[:, part] * cos_twist - imag[:, part] * sin_twist,
                real[:, part] * sin_twist + imag[:, part] * cos_twist,
                table_ref,
                FORWARD_SECOND,
            )
            for part in lanes
        ]

    def multiply(spectra):
        (fr, fi), (ar, ai), (br, bi), (mr, mi) = spectra
        products = [
            (fr * ar - fi * ai, fr * ai + fi * ar),
            (fr * br - fi * bi, fr * bi + fi * br),
            (fr * mr + fi * mi, fr * mi - fi * mr),
            (mr * br + mi * bi, mi * br - mr * bi),
        ]
        return [two_pass(real, imag, table_ref, INVERSE_SECOND) for real, imag in products]

    def store(step, results):
        sum_twist = twist_ref[rows_of(step), 2 * SECOND : 3 * SECOND]
        difference_twist = twist_ref[rows_of(step), 3 * SECOND :]
        for part, (real, imag) in zip(lanes, results):
            sum_ref[rows_of(step), part] = (real * difference_twist + imag * sum_twist).astype(BF16)
            difference_ref[rows_of(step), part] = (real * sum_twist - imag * difference_twist).astype(BF16)

    step = HALF // 2
    count = step // ROWS
    early = rows_of(STEPS - 2).stop

    def way_back(part, rows):
        columns = slice(BACK + rows.start, BACK + rows.stop)
        even = jnp.dot(
            table_ref[part * step : (part + 1) * step, columns], sum_ref[rows, :], preferred_element_type=F32
        )
        odd = jnp.dot(
            table_ref[HALF + part * step : HALF + (part + 1) * step, columns],
            difference_ref[rows, :],
            preferred_element_type=F32,
        )
        return even, odd

    turned, spectra, results, partial = {}, {}, {}, {}

    def begin(double, pair):
        for index, value in enumerate(first_factor(double, pair)):
            turned.setdefault(2 * double + index, []).append(value)

    for pair in range(2):
        lay_out(pair)
        begin(0, pair)
    for turn in range(1, STEPS + 3):
        if 0 <= turn - 3 < STEPS:
            store(turn - 3, results.pop(turn - 3))
        if turn > STEPS:
            partial[turn - STEPS - 1] = way_back(turn - STEPS - 1, slice(0, early))
        if 0 <= turn - 2 < STEPS:
            results[turn - 2] = multiply(spectra.pop(turn - 2))
        if 0 <= turn - 1 < STEPS:
            spectra[turn - 1] = second_factor(turn - 1, turned.pop(turn - 1))
        if turn % 2 and turn + 1 < STEPS:
            for pair in range(2):
                begin((turn + 1) // 2, pair)

    for part in range(HALF // step):
        even, odd = way_back(part, slice(early, FIRST))
        even, odd = even + partial[part][0], odd + partial[part][1]
        for result, places in (
            (even + odd, range(part * count, (part + 1) * count)),
            (even - odd, range(LANES - 1 - part * count, LANES - 1 - (part + 1) * count, -1)),
        ):
            pieces = [result[:, lane].reshape(count, ROWS, LANES) for lane in lanes]
            joined = jnp.concatenate(pieces, axis=1).astype(BF16)
            for index, place in enumerate(places):
                out_ref[place] = joined[index]


def vmem():
    return pl.BlockSpec(memory_space=pltpu.VMEM)


def hbm():
    return pl.BlockSpec(memory_space=pltpu.HBM)


def exchange(pieces):
    return lax.all_to_all(pieces, AXES, split_axis=0, concat_axis=0, tiled=True)


def on_device(signal_first, gate_first, signal_second, gate_second, upstream_second, filter_param):
    positions = ROWS * LANES
    local = jax.ShapeDtypeStruct((positions, LANES), BF16)
    pieces = jax.ShapeDtypeStruct((LANES, PIECE, LANES), BF16)
    sources = (filter_param, signal_first, signal_second, gate_second, upstream_second)
    packed = pl.pallas_call(
        pack_kernel,
        out_shape=pieces,
        in_specs=[hbm()] * 5,
        out_specs=vmem(),
        scratch_shapes=[
            pltpu.VMEM((5, positions, LANES), BF16),
            pltpu.VMEM((ARRAYS, STRIDE * LANES + PAIR, LANES), F32),
            pltpu.SemaphoreType.DMA((5,)),
        ],
        compiler_params=pltpu.CompilerParams(vmem_limit_bytes=40 * 1024 * 1024),
        cost_estimate=pl.CostEstimate(flops=20_000_000_000, bytes_accessed=2_400_000, transcendentals=0),
        name="pack",
    )(*[pltpu.with_memory_space_constraint(value, pltpu.HBM) for value in sources])
    convolved = pl.pallas_call(
        convolve_kernel,
        out_shape=pieces,
        in_specs=[vmem()] * 3,
        out_specs=vmem(),
        scratch_shapes=[pltpu.VMEM((ARRAYS, FIRST + PAIR, LANES), F32)]
        + [pltpu.VMEM((FIRST, ARRAYS * LANES), BF16)] * 3,
        compiler_params=pltpu.CompilerParams(vmem_limit_bytes=40 * 1024 * 1024),
        name="convolve",
    )(exchange(packed), *make_tables())
    return pl.pallas_call(
        unpack_kernel,
        out_shape=(local, local, local, jax.ShapeDtypeStruct((positions, LANES), F32)),
        in_specs=[vmem()] * 3,
        out_specs=(hbm(),) * 4,
        scratch_shapes=[
            pltpu.VMEM((ARRAYS, STRIDE * LANES + PAIR, LANES), F32),
            pltpu.VMEM((3, positions, LANES), BF16),
            pltpu.VMEM((positions, LANES), F32),
            pltpu.SemaphoreType.DMA((ARRAYS,)),
        ],
        compiler_params=pltpu.CompilerParams(vmem_limit_bytes=40 * 1024 * 1024),
        name="unpack",
    )(exchange(convolved), gate_first, upstream_second)


def solution(mesh):
    spec = P(AXES, None)
    return jax.shard_map(
        on_device,
        mesh=mesh,
        in_specs=(spec,) * 6,
        out_specs=(spec,) * 4,
        check_vma=False,
    )
```

```python
import functools
import math

import jax
import jax.numpy as jnp
import ml_dtypes
import numpy as np
from jax import lax
from jax.experimental import pallas as pl
from jax.experimental.pallas import tpu as pltpu
from jax.sharding import PartitionSpec as P

AXES = ("ctx", "tp", "dp")
SEQ = 131072
ROWS = 8
LANES = 128
FIRST = 1024
SECOND = 128
HALF = FIRST // 2
QUARTER = FIRST // 4
CHUNK = 64
STEPS = QUARTER // CHUNK
BLOCK = 4 * CHUNK
ARRAYS = 4
PIECE = ARRAYS * ROWS
PAIR = 2 * ROWS
STRIDE = ROWS + 1
BACK = FIRST
FORWARD_SECOND = BACK + FIRST
INVERSE_SECOND = FORWARD_SECOND + 2 * SECOND
TABLE_WIDTH = INVERSE_SECOND + 2 * SECOND
SECOND_SCALE = 1.66569
BF16 = jnp.bfloat16
F32 = jnp.float32


@functools.cache
def make_tables():
    quarter = QUARTER * np.arange(4).reshape(1, 4, 1)
    first = (np.arange(QUARTER).reshape(STEPS, 1, CHUNK) + quarter).reshape(FIRST)
    position, second = np.arange(FIRST), np.arange(SECOND)
    product = (4 * first[:, None] + 1) * (2 * position[None, :] + 1) % (8 * FIRST)
    first_phase = 2 * np.pi * product / (8 * FIRST)
    twist_phase = 2 * np.pi * (4 * first[:, None] + 1) * (second[None, :] - SECOND // 2) / (4 * SEQ)
    forward_phase = twist_phase + np.pi / 4 * (first // QUARTER)[:, None]
    second_phase = 2 * np.pi * ((second[:, None] * second[None, :]) % SECOND) / SECOND
    scale = (SEQ * math.sqrt(SEQ) * SECOND_SCALE**3 * math.sqrt(2.0)) ** (-1 / 3)
    back = [np.cos(twist_phase) + np.sin(twist_phase), np.cos(twist_phase) - np.sin(twist_phase)]
    twist = scale * np.concatenate([np.cos(forward_phase), np.sin(forward_phase)] + back, axis=1)
    cos_second, sin_second = np.cos(second_phase), np.sin(second_phase)
    forward_second = np.block([[cos_second, sin_second], [-sin_second, cos_second]])
    inverse_second = np.block([[cos_second, -sin_second], [sin_second, cos_second]])

    columns = position.reshape(QUARTER, 4).T.reshape(FIRST)
    lowest = first_phase.reshape(STEPS // 2, 2, 4, CHUNK, FIRST)[:, :, 0].reshape(STEPS // 2, 2 * CHUNK, FIRST)
    lowest = lowest[:, :, columns]
    joined = np.zeros((FIRST, TABLE_WIDTH), ml_dtypes.bfloat16)
    joined[:HALF, :FIRST] = np.concatenate([np.cos(lowest), np.sin(lowest)], axis=1).reshape(HALF, FIRST)
    half_phase = first_phase[:, :HALF].T
    joined[:HALF, BACK : BACK + FIRST] = np.cos(half_phase - np.pi / 4)
    joined[HALF:, BACK : BACK + FIRST] = np.cos(half_phase + np.pi / 4)
    for column, table in ((FORWARD_SECOND, forward_second), (INVERSE_SECOND, inverse_second)):
        table = SECOND_SCALE * np.concatenate([table, table], axis=0)
        joined[: 4 * SECOND, column : column + 2 * SECOND] = table
    return joined, twist.astype(np.float32)


def pack_kernel(filter_hbm, first_hbm, second_hbm, gate_hbm, upstream_hbm, out_ref, local, scratch, sems):
    sources = (filter_hbm, first_hbm, second_hbm, gate_hbm, upstream_hbm)
    copies = [
        pltpu.make_async_copy(source, local.at[index], sems.at[index])
        for index, source in enumerate(sources)
    ]
    for copy in copies:
        copy.start()
    for index in range(ARRAYS):
        if index % 2 == 0:
            for copy in copies[:2] if index == 0 else copies[2:]:
                copy.wait()
        for row in range(ROWS):
            span = pl.ds(row * LANES, LANES)
            block = local[index, span, :]
            if index == ARRAYS - 1:
                block = (block.astype(F32) * local[ARRAYS, span, :].astype(F32)).astype(BF16)
            scratch[index, pl.ds(row, LANES, stride=STRIDE), :] = block.T.astype(F32)
        if index % 2:
            for channel in range(LANES):
                rows = pl.ds(channel * STRIDE, ROWS)
                pair = jnp.concatenate([scratch[index - 1, rows, :], scratch[index, rows, :]], axis=0)
                out_ref[channel, index // 2 * PAIR : (index // 2 + 1) * PAIR, :] = pair.astype(BF16)


def unpack_kernel(
    in_ref, gate_ref, upstream_ref, mixed_hbm, signal_hbm, gate_out_hbm, filter_hbm,
    scratch, halves, filter_out, sems,
):
    mirrored = lax.axis_index("ctx") >= lax.axis_size("ctx") // 2
    targets = (mixed_hbm, gate_out_hbm, signal_hbm, filter_hbm)
    copies = []
    for index in (3, 2, 0, 1):
        if index in (3, 0):
            for channel in range(LANES):
                pair = in_ref[channel, index // 2 * PAIR : (index // 2 + 1) * PAIR, :].astype(F32)
                rows = pl.ds(channel * STRIDE, ROWS)
                scratch[index // 2 * 2, rows, :] = pair[:ROWS]
                scratch[index // 2 * 2 + 1, rows, :] = pair[ROWS:]
        for row in range(ROWS):
            place = jnp.where(mirrored, ROWS - 1 - row, row)
            span = pl.ds(pl.multiple_of(place * LANES, LANES), LANES)
            block = scratch[index, pl.ds(row, LANES, stride=STRIDE), :]
            block = block.astype(BF16).T.astype(F32)
            if index == 0:
                halves[index, span, :] = (gate_ref[span, :].astype(F32) * block).astype(BF16)
            elif index == 1:
                halves[index, span, :] = (upstream_ref[span, :].astype(F32) * block).astype(BF16)
            elif index == 2:
                halves[index, span, :] = block.astype(BF16)
            else:
                filter_out[span, :] = block
        source = filter_out if index == 3 else halves.at[index]
        copies.append(pltpu.make_async_copy(source, targets[index], sems.at[index]))
        if index in (2, 1):
            for copy in copies[-2:]:
                copy.start()
    for copy in copies:
        copy.wait()


def two_pass(real, imag, table_ref, column):
    real_high, imag_high = real.astype(BF16), imag.astype(BF16)
    real_low = (real - real_high.astype(F32)).astype(BF16)
    imag_low = (imag - imag_high.astype(F32)).astype(BF16)
    joined = jnp.concatenate([real_high, imag_high, real_low, imag_low], axis=1)
    table = table_ref[: 4 * SECOND, column : column + 2 * SECOND]
    out = jnp.dot(joined, table, preferred_element_type=F32)
    return out[:, :SECOND], out[:, SECOND:]


def convolve_kernel(in_ref, table_ref, twist_ref, out_ref, rows_ref, values_ref, sum_ref, difference_ref):
    lanes = [slice(index * LANES, (index + 1) * LANES) for index in range(ARRAYS)]
    pairs = [slice(start, start + 2 * LANES) for start in range(0, ARRAYS * LANES, 2 * LANES)]

    def lay_out(pair):
        arrived = in_ref[:, pair * PAIR : (pair + 1) * PAIR, :].astype(F32)
        for index in range(2):
            part = lanes[2 * pair + index]
            rows_ref[2 * pair + index, :FIRST, :] = arrived[:, index * ROWS : (index + 1) * ROWS, :].reshape(FIRST, LANES)
            for residue in range(4):
                values_ref[residue * QUARTER : (residue + 1) * QUARTER, part] = (
                    rows_ref[2 * pair + index, pl.ds(residue, QUARTER, stride=4), :].astype(BF16)
                )

    def rows_of(step):
        return slice(step * BLOCK, (step + 1) * BLOCK)

    def first_factor(double, pair):
        rows = rows_of(double)
        p0, p1, p2, p3 = (
            jnp.dot(
                table_ref[rows, residue * QUARTER : (residue + 1) * QUARTER],
                values_ref[residue * QUARTER : (residue + 1) * QUARTER, pairs[pair]],
                preferred_element_type=F32,
            )
            for residue in range(4)
        )
        s02, d02, s13, d13 = p0 + p2, p0 - p2, p1 + p3, p1 - p3
        real, imag = slice(0, 2 * CHUNK), slice(2 * CHUNK, 4 * CHUNK)
        reals = [s02[real] + s13[real], d02[real] - d13[imag], s02[real] - s13[real], d02[real] + d13[imag]]
        imags = [s02[imag] + s13[imag], d02[imag] + d13[real], s02[imag] - s13[imag], d02[imag] - d13[real]]
        return [
            tuple(
                jnp.concatenate([value[step * CHUNK : (step + 1) * CHUNK] for value in values], axis=0)
                for values in (reals, imags)
            )
            for step in range(2)
        ]

    def second_factor(step, turned):
        real, imag = (jnp.concatenate(parts, axis=1) for parts in zip(*turned))
        cos_twist, sin_twist = twist_ref[rows_of(step), :SECOND], twist_ref[rows_of(step), SECOND : 2 * SECOND]
        return [
            two_pass(
                real[:, part] * cos_twist - imag[:, part] * sin_twist,
                real[:, part] * sin_twist + imag[:, part] * cos_twist,
                table_ref,
                FORWARD_SECOND,
            )
            for part in lanes
        ]

    def multiply(spectra):
        (fr, fi), (ar, ai), (br, bi), (mr, mi) = spectra
        products = [
            (fr * ar - fi * ai, fr * ai + fi * ar),
            (fr * br - fi * bi, fr * bi + fi * br),
            (fr * mr + fi * mi, fr * mi - fi * mr),
            (mr * br + mi * bi, mi * br - mr * bi),
        ]
        return [two_pass(real, imag, table_ref, INVERSE_SECOND) for real, imag in products]

    def store(step, results):
        sum_twist = twist_ref[rows_of(step), 2 * SECOND : 3 * SECOND]
        difference_twist = twist_ref[rows_of(step), 3 * SECOND :]
        for part, (real, imag) in zip(lanes, results):
            sum_ref[rows_of(step), part] = (real * difference_twist + imag * sum_twist).astype(BF16)
            difference_ref[rows_of(step), part] = (real * sum_twist - imag * difference_twist).astype(BF16)

    step = HALF // 4
    count = step // ROWS
    early = rows_of(STEPS - 2).stop

    def way_back(part, rows):
        columns = slice(BACK + rows.start, BACK + rows.stop)
        even = jnp.dot(
            table_ref[part * step : (part + 1) * step, columns], sum_ref[rows, :], preferred_element_type=F32
        )
        odd = jnp.dot(
            table_ref[HALF + part * step : HALF + (part + 1) * step, columns],
            difference_ref[rows, :],
            preferred_element_type=F32,
        )
        return even, odd

    turned, spectra, results, partial = {}, {}, {}, {}

    def begin(double, pair):
        for index, value in enumerate(first_factor(double, pair)):
            turned.setdefault(2 * double + index, []).append(value)

    for pair in range(2):
        lay_out(pair)
        begin(0, pair)
    for turn in range(1, STEPS + 1):
        if turn >= 3:
            store(turn - 3, results.pop(turn - 3))
        if turn >= 2:
            results[turn - 2] = multiply(spectra.pop(turn - 2))
        spectra[turn - 1] = second_factor(turn - 1, turned.pop(turn - 1))
        if turn % 2 and turn + 1 < STEPS:
            for pair in range(2):
                begin((turn + 1) // 2, pair)
    results[STEPS - 1] = multiply(spectra.pop(STEPS - 1))
    for last in (STEPS - 2, STEPS - 1):
        store(last, results.pop(last))
        for part in range(2 * (last - STEPS + 2), 2 * (last - STEPS + 3)):
            partial[part] = way_back(part, slice(0, early))

    for part in range(HALF // step):
        even, odd = way_back(part, slice(early, FIRST))
        even, odd = even + partial[part][0], odd + partial[part][1]
        for result, places in (
            (even + odd, range(part * count, (part + 1) * count)),
            (even - odd, range(LANES - 1 - part * count, LANES - 1 - (part + 1) * count, -1)),
        ):
            pieces = [result[:, lane].reshape(count, ROWS, LANES) for lane in lanes]
            joined = jnp.concatenate(pieces, axis=1).astype(BF16)
            for index, place in enumerate(places):
                out_ref[place] = joined[index]


def vmem():
    return pl.BlockSpec(memory_space=pltpu.VMEM)


def hbm():
    return pl.BlockSpec(memory_space=pltpu.HBM)


def exchange(pieces):
    return lax.all_to_all(pieces, AXES, split_axis=0, concat_axis=0, tiled=True)


def on_device(signal_first, gate_first, signal_second, gate_second, upstream_second, filter_param):
    positions = ROWS * LANES
    local = jax.ShapeDtypeStruct((positions, LANES), BF16)
    pieces = jax.ShapeDtypeStruct((LANES, PIECE, LANES), BF16)
    sources = (filter_param, signal_first, signal_second, gate_second, upstream_second)
    packed = pl.pallas_call(
        pack_kernel,
        out_shape=pieces,
        in_specs=[hbm()] * 5,
        out_specs=vmem(),
        scratch_shapes=[
            pltpu.VMEM((5, positions, LANES), BF16),
            pltpu.VMEM((ARRAYS, STRIDE * LANES + PAIR, LANES), F32),
            pltpu.SemaphoreType.DMA((5,)),
        ],
        compiler_params=pltpu.CompilerParams(vmem_limit_bytes=40 * 1024 * 1024),
        cost_estimate=pl.CostEstimate(flops=20_000_000_000, bytes_accessed=2_400_000, transcendentals=0),
        name="pack",
    )(*[pltpu.with_memory_space_constraint(value, pltpu.HBM) for value in sources])
    convolved = pl.pallas_call(
        convolve_kernel,
        out_shape=pieces,
        in_specs=[vmem()] * 3,
        out_specs=vmem(),
        scratch_shapes=[pltpu.VMEM((ARRAYS, FIRST + PAIR, LANES), F32)]
        + [pltpu.VMEM((FIRST, ARRAYS * LANES), BF16)] * 3,
        compiler_params=pltpu.CompilerParams(vmem_limit_bytes=40 * 1024 * 1024),
        name="convolve",
    )(exchange(packed), *make_tables())
    return pl.pallas_call(
        unpack_kernel,
        out_shape=(local, local, local, jax.ShapeDtypeStruct((positions, LANES), F32)),
        in_specs=[vmem()] * 3,
        out_specs=(hbm(),) * 4,
        scratch_shapes=[
            pltpu.VMEM((ARRAYS, STRIDE * LANES + PAIR, LANES), F32),
            pltpu.VMEM((3, positions, LANES), BF16),
            pltpu.VMEM((positions, LANES), F32),
            pltpu.SemaphoreType.DMA((ARRAYS,)),
        ],
        compiler_params=pltpu.CompilerParams(vmem_limit_bytes=40 * 1024 * 1024),
        name="unpack",
    )(exchange(convolved), gate_first, upstream_second)


def solution(mesh):
    spec = P(AXES, None)
    return jax.shard_map(
        on_device,
        mesh=mesh,
        in_specs=(spec,) * 6,
        out_specs=(spec,) * 4,
        check_vma=False,
    )
```

```python
import functools
import math

import jax
import jax.numpy as jnp
import ml_dtypes
import numpy as np
from jax import lax
from jax.experimental import pallas as pl
from jax.experimental.pallas import tpu as pltpu
from jax.sharding import PartitionSpec as P

AXES = ("ctx", "tp", "dp")
SEQ = 131072
ROWS = 8
LANES = 128
FIRST = 1024
SECOND = 128
HALF = FIRST // 2
QUARTER = FIRST // 4
CHUNK = 64
STEPS = QUARTER // CHUNK
BLOCK = 4 * CHUNK
ARRAYS = 4
PIECE = ARRAYS * ROWS
PAIR = 2 * ROWS
STRIDE = ROWS + 1
BACK = FIRST
FORWARD_SECOND = BACK + FIRST
INVERSE_SECOND = FORWARD_SECOND + 2 * SECOND
TABLE_WIDTH = INVERSE_SECOND + 2 * SECOND
SECOND_SCALE = 1.66569
BF16 = jnp.bfloat16
F32 = jnp.float32


@functools.cache
def make_tables():
    quarter = QUARTER * np.arange(4).reshape(1, 4, 1)
    first = (np.arange(QUARTER).reshape(STEPS, 1, CHUNK) + quarter).reshape(FIRST)
    position, second = np.arange(FIRST), np.arange(SECOND)
    product = (4 * first[:, None] + 1) * (2 * position[None, :] + 1) % (8 * FIRST)
    first_phase = 2 * np.pi * product / (8 * FIRST)
    twist_phase = 2 * np.pi * (4 * first[:, None] + 1) * (second[None, :] - SECOND // 2) / (4 * SEQ)
    forward_phase = twist_phase + np.pi / 4 * (first // QUARTER)[:, None]
    second_phase = 2 * np.pi * ((second[:, None] * second[None, :]) % SECOND) / SECOND
    scale = (SEQ * math.sqrt(SEQ) * SECOND_SCALE**3 * math.sqrt(2.0)) ** (-1 / 3)
    back = [np.cos(twist_phase) + np.sin(twist_phase), np.cos(twist_phase) - np.sin(twist_phase)]
    twist = scale * np.concatenate([np.cos(forward_phase), np.sin(forward_phase)] + back, axis=1)
    cos_second, sin_second = np.cos(second_phase), np.sin(second_phase)
    forward_second = np.block([[cos_second, sin_second], [-sin_second, cos_second]])
    inverse_second = np.block([[cos_second, -sin_second], [sin_second, cos_second]])

    columns = position.reshape(QUARTER, 4).T.reshape(FIRST)
    lowest = first_phase.reshape(STEPS // 2, 2, 4, CHUNK, FIRST)[:, :, 0].reshape(STEPS // 2, 2 * CHUNK, FIRST)
    lowest = lowest[:, :, columns]
    joined = np.zeros((FIRST, TABLE_WIDTH), ml_dtypes.bfloat16)
    joined[:HALF, :FIRST] = np.concatenate([np.cos(lowest), np.sin(lowest)], axis=1).reshape(HALF, FIRST)
    half_phase = first_phase[:, :HALF].T
    joined[:HALF, BACK : BACK + FIRST] = np.cos(half_phase - np.pi / 4)
    joined[HALF:, BACK : BACK + FIRST] = np.cos(half_phase + np.pi / 4)
    for column, table in ((FORWARD_SECOND, forward_second), (INVERSE_SECOND, inverse_second)):
        table = SECOND_SCALE * np.concatenate([table, table], axis=0)
        joined[: 4 * SECOND, column : column + 2 * SECOND] = table
    return joined, twist.astype(np.float32)


def pack_kernel(filter_hbm, first_hbm, second_hbm, gate_hbm, upstream_hbm, out_ref, local, scratch, sems):
    sources = (filter_hbm, first_hbm, second_hbm, gate_hbm, upstream_hbm)
    copies = [
        pltpu.make_async_copy(source, local.at[index], sems.at[index])
        for index, source in enumerate(sources)
    ]
    for copy in copies:
        copy.start()
    for index in range(ARRAYS):
        if index % 2 == 0:
            for copy in copies[:2] if index == 0 else copies[2:]:
                copy.wait()
        for row in range(ROWS):
            span = pl.ds(row * LANES, LANES)
            block = local[index, span, :]
            if index == ARRAYS - 1:
                block = (block.astype(F32) * local[ARRAYS, span, :].astype(F32)).astype(BF16)
            scratch[index, pl.ds(row, LANES, stride=STRIDE), :] = block.T.astype(F32)
        if index % 2:
            for channel in range(LANES):
                rows = pl.ds(channel * STRIDE, ROWS)
                pair = jnp.concatenate([scratch[index - 1, rows, :], scratch[index, rows, :]], axis=0)
                out_ref[channel, index // 2 * PAIR : (index // 2 + 1) * PAIR, :] = pair.astype(BF16)


def unpack_kernel(
    in_ref, gate_ref, upstream_ref, mixed_hbm, signal_hbm, gate_out_hbm, filter_hbm,
    scratch, halves, filter_out, sems,
):
    mirrored = lax.axis_index("ctx") >= lax.axis_size("ctx") // 2
    targets = (mixed_hbm, gate_out_hbm, signal_hbm, filter_hbm)
    copies = []
    for index in (3, 2, 0, 1):
        if index in (3, 0):
            for channel in range(LANES):
                pair = in_ref[channel, index // 2 * PAIR : (index // 2 + 1) * PAIR, :].astype(F32)
                rows = pl.ds(channel * STRIDE, ROWS)
                scratch[index // 2 * 2, rows, :] = pair[:ROWS]
                scratch[index // 2 * 2 + 1, rows, :] = pair[ROWS:]
        for row in range(ROWS):
            place = jnp.where(mirrored, ROWS - 1 - row, row)
            span = pl.ds(pl.multiple_of(place * LANES, LANES), LANES)
            block = scratch[index, pl.ds(row, LANES, stride=STRIDE), :]
            block = block.astype(BF16).T.astype(F32)
            if index == 0:
                halves[index, span, :] = (gate_ref[span, :].astype(F32) * block).astype(BF16)
            elif index == 1:
                halves[index, span, :] = (upstream_ref[span, :].astype(F32) * block).astype(BF16)
            elif index == 2:
                halves[index, span, :] = block.astype(BF16)
            else:
                filter_out[span, :] = block
        source = filter_out if index == 3 else halves.at[index]
        copies.append(pltpu.make_async_copy(source, targets[index], sems.at[index]))
        if index in (2, 1):
            for copy in copies[-2:]:
                copy.start()
    for copy in copies:
        copy.wait()


def two_pass(real, imag, table_ref, column):
    real_high, imag_high = real.astype(BF16), imag.astype(BF16)
    real_low = (real - real_high.astype(F32)).astype(BF16)
    imag_low = (imag - imag_high.astype(F32)).astype(BF16)
    joined = jnp.concatenate([real_high, imag_high, real_low, imag_low], axis=1)
    table = table_ref[: 4 * SECOND, column : column + 2 * SECOND]
    out = jnp.dot(joined, table, preferred_element_type=F32)
    return out[:, :SECOND], out[:, SECOND:]


def convolve_kernel(in_ref, table_ref, twist_ref, out_ref, rows_ref, values_ref, sum_ref, difference_ref):
    lanes = [slice(index * LANES, (index + 1) * LANES) for index in range(ARRAYS)]
    pairs = [slice(start, start + 2 * LANES) for start in range(0, ARRAYS * LANES, 2 * LANES)]

    def lay_out(pair):
        arrived = in_ref[:, pair * PAIR : (pair + 1) * PAIR, :].astype(F32)
        for index in range(2):
            part = lanes[2 * pair + index]
            rows_ref[2 * pair + index, :FIRST, :] = arrived[:, index * ROWS : (index + 1) * ROWS, :].reshape(FIRST, LANES)
            for residue in range(4):
                values_ref[residue * QUARTER : (residue + 1) * QUARTER, part] = (
                    rows_ref[2 * pair + index, pl.ds(residue, QUARTER, stride=4), :].astype(BF16)
                )

    def rows_of(step):
        return slice(step * BLOCK, (step + 1) * BLOCK)

    def first_factor(double, pair):
        rows = rows_of(double)
        p0, p1, p2, p3 = (
            jnp.dot(
                table_ref[rows, residue * QUARTER : (residue + 1) * QUARTER],
                values_ref[residue * QUARTER : (residue + 1) * QUARTER, pairs[pair]],
                preferred_element_type=F32,
            )
            for residue in range(4)
        )
        s02, d02, s13, d13 = p0 + p2, p0 - p2, p1 + p3, p1 - p3
        real, imag = slice(0, 2 * CHUNK), slice(2 * CHUNK, 4 * CHUNK)
        reals = [s02[real] + s13[real], d02[real] - d13[imag], s02[real] - s13[real], d02[real] + d13[imag]]
        imags = [s02[imag] + s13[imag], d02[imag] + d13[real], s02[imag] - s13[imag], d02[imag] - d13[real]]
        return [
            tuple(
                jnp.concatenate([value[step * CHUNK : (step + 1) * CHUNK] for value in values], axis=0)
                for values in (reals, imags)
            )
            for step in range(2)
        ]

    def second_factor(step, turned):
        real, imag = (jnp.concatenate(parts, axis=1) for parts in zip(*turned))
        cos_twist, sin_twist = twist_ref[rows_of(step), :SECOND], twist_ref[rows_of(step), SECOND : 2 * SECOND]
        return [
            two_pass(
                real[:, part] * cos_twist - imag[:, part] * sin_twist,
                real[:, part] * sin_twist + imag[:, part] * cos_twist,
                table_ref,
                FORWARD_SECOND,
            )
            for part in lanes
        ]

    def multiply(spectra):
        (fr, fi), (ar, ai), (br, bi), (mr, mi) = spectra
        products = [
            (fr * ar - fi * ai, fr * ai + fi * ar),
            (fr * br - fi * bi, fr * bi + fi * br),
            (fr * mr + fi * mi, fr * mi - fi * mr),
            (mr * br + mi * bi, mi * br - mr * bi),
        ]
        return [two_pass(real, imag, table_ref, INVERSE_SECOND) for real, imag in products]

    def store(step, results):
        sum_twist = twist_ref[rows_of(step), 2 * SECOND : 3 * SECOND]
        difference_twist = twist_ref[rows_of(step), 3 * SECOND :]
        for part, (real, imag) in zip(lanes, results):
            sum_ref[rows_of(step), part] = (real * difference_twist + imag * sum_twist).astype(BF16)
            difference_ref[rows_of(step), part] = (real * sum_twist - imag * difference_twist).astype(BF16)

    step = HALF // 4
    count = step // ROWS
    early = rows_of(STEPS - 2).stop

    def way_back(part, rows):
        columns = slice(BACK + rows.start, BACK + rows.stop)
        even = jnp.dot(
            table_ref[part * step : (part + 1) * step, columns], sum_ref[rows, :], preferred_element_type=F32
        )
        odd = jnp.dot(
            table_ref[HALF + part * step : HALF + (part + 1) * step, columns],
            difference_ref[rows, :],
            preferred_element_type=F32,
        )
        return even, odd

    turned, spectra, results, partial = {}, {}, {}, {}

    def begin(double, pair):
        for index, value in enumerate(first_factor(double, pair)):
            turned.setdefault(2 * double + index, []).append(value)

    for pair in range(2):
        lay_out(pair)
        for double in range(STEPS // 2):
            begin(double, pair)
    for turn in range(1, STEPS + 3):
        if 0 <= turn - 3 < STEPS:
            store(turn - 3, results.pop(turn - 3))
        if turn > STEPS:
            for part in range(2 * (turn - STEPS - 1), 2 * (turn - STEPS)):
                partial[part] = way_back(part, slice(0, early))
        if 0 <= turn - 2 < STEPS:
            results[turn - 2] = multiply(spectra.pop(turn - 2))
        if 0 <= turn - 1 < STEPS:
            spectra[turn - 1] = second_factor(turn - 1, turned.pop(turn - 1))

    for part in range(HALF // step):
        even, odd = way_back(part, slice(early, FIRST))
        even, odd = even + partial[part][0], odd + partial[part][1]
        for result, places in (
            (even + odd, range(part * count, (part + 1) * count)),
            (even - odd, range(LANES - 1 - part * count, LANES - 1 - (part + 1) * count, -1)),
        ):
            pieces = [result[:, lane].reshape(count, ROWS, LANES) for lane in lanes]
            joined = jnp.concatenate(pieces, axis=1).astype(BF16)
            for index, place in enumerate(places):
                out_ref[place] = joined[index]


def vmem():
    return pl.BlockSpec(memory_space=pltpu.VMEM)


def hbm():
    return pl.BlockSpec(memory_space=pltpu.HBM)


def exchange(pieces):
    return lax.all_to_all(pieces, AXES, split_axis=0, concat_axis=0, tiled=True)


def on_device(signal_first, gate_first, signal_second, gate_second, upstream_second, filter_param):
    positions = ROWS * LANES
    local = jax.ShapeDtypeStruct((positions, LANES), BF16)
    pieces = jax.ShapeDtypeStruct((LANES, PIECE, LANES), BF16)
    sources = (filter_param, signal_first, signal_second, gate_second, upstream_second)
    packed = pl.pallas_call(
        pack_kernel,
        out_shape=pieces,
        in_specs=[hbm()] * 5,
        out_specs=vmem(),
        scratch_shapes=[
            pltpu.VMEM((5, positions, LANES), BF16),
            pltpu.VMEM((ARRAYS, STRIDE * LANES + PAIR, LANES), F32),
            pltpu.SemaphoreType.DMA((5,)),
        ],
        compiler_params=pltpu.CompilerParams(vmem_limit_bytes=40 * 1024 * 1024),
        cost_estimate=pl.CostEstimate(flops=20_000_000_000, bytes_accessed=2_400_000, transcendentals=0),
        name="pack",
    )(*[pltpu.with_memory_space_constraint(value, pltpu.HBM) for value in sources])
    convolved = pl.pallas_call(
        convolve_kernel,
        out_shape=pieces,
        in_specs=[vmem()] * 3,
        out_specs=vmem(),
        scratch_shapes=[pltpu.VMEM((ARRAYS, FIRST + PAIR, LANES), F32)]
        + [pltpu.VMEM((FIRST, ARRAYS * LANES), BF16)] * 3,
        compiler_params=pltpu.CompilerParams(vmem_limit_bytes=40 * 1024 * 1024),
        name="convolve",
    )(exchange(packed), *make_tables())
    return pl.pallas_call(
        unpack_kernel,
        out_shape=(local, local, local, jax.ShapeDtypeStruct((positions, LANES), F32)),
        in_specs=[vmem()] * 3,
        out_specs=(hbm(),) * 4,
        scratch_shapes=[
            pltpu.VMEM((ARRAYS, STRIDE * LANES + PAIR, LANES), F32),
            pltpu.VMEM((3, positions, LANES), BF16),
            pltpu.VMEM((positions, LANES), F32),
            pltpu.SemaphoreType.DMA((ARRAYS,)),
        ],
        compiler_params=pltpu.CompilerParams(vmem_limit_bytes=40 * 1024 * 1024),
        name="unpack",
    )(exchange(convolved), gate_first, upstream_second)


def solution(mesh):
    spec = P(AXES, None)
    return jax.shard_map(
        on_device,
        mesh=mesh,
        in_specs=(spec,) * 6,
        out_specs=(spec,) * 4,
        check_vma=False,
    )
```
